128 devices in a mesh: pipe: 4 (over z_lo, core), fsdp: 32 (over z_hi, x, y).
Axes of the slice: x: 4, y: 4, z: 4 (z_hi: 2, z_lo: 2; z = z_hi * 2 + z_lo), core: 2. Of those that a mesh axis runs over, the one named last changes fastest.
Arguments:
- entering: bfloat16 [3, 2048, 8192], P(None, 'fsdp'), may hold values from -6 to 6
- in_store: bfloat16 [4, 3, 2048, 8192], P('pipe', None, 'fsdp'), may hold values from -6 to 6
- out_store: bfloat16 [4, 3, 2048, 8192], P('pipe', None, 'fsdp'), may hold values from -6 to 6
- norm_gain: bfloat16 [4, 8192], P('pipe', 'fsdp'), may hold values from 0.25 to 1.75
- adapter_down: bfloat16 [4, 8192, 256], P('pipe', 'fsdp'), may hold values from -0.0625 to 0.0625
- adapter_up: bfloat16 [4, 256, 8192], P('pipe', None, 'fsdp'), may hold values from -0.375 to 0.375
- sample_ids: int32 [3], replicated, may hold values from 0 to 2, each once
- cotangent: bfloat16 [3, 2048, 8192], P(None, 'fsdp'), may hold values from -6 to 6
Outputs:
- sent_refresh: bfloat16 [4, 3, 2048, 8192], P('pipe', None, 'fsdp')
- section_inputs: bfloat16 [4, 3, 2048, 8192], P('pipe', None, 'fsdp')
- input_grads: bfloat16 [4, 3, 2048, 8192], P('pipe', None, 'fsdp')
- grad_gain: float32 [4, 8192], P('pipe', 'fsdp')
- grad_down: float32 [4, 8192, 256], P('pipe', 'fsdp')
- grad_up: float32 [4, 256, 8192], P('pipe', None, 'fsdp')
The draws below stay inside these ranges and needn't reach their ends.
Inputs may be any that keep to these rules, and one draw needn't show every extreme that they name: `sample_ids`: each micro-batch names a different stored sample.
All inputs are finite; a program needn't handle non-finite values. Where the reference program divides by a largest or mean magnitude, that divisor is 1e-20 or more.
Results may differ from the reference program's by a relative error of at most 0.04.
Values may be sent and summed in bfloat16 or wider, within the bound.
No kernel may reach another device: no remote copies, remote signals or barrier semaphores. Data moves between devices by JAX's collectives and lax.ppermute only.
A program may use at most 192 MiB of HBM per device.

```python
import jax
import jax.numpy as jnp
from jax import lax

D = 8192
R = 256
M = 3
L = 2048
N_PIPE = 4
N_FSDP = 32


def levels(key, shape, shards, least, high):
    def one(position, shards_of):
        heights = jax.random.uniform(jax.random.fold_in(jax.random.fold_in(key, 6), position), (shards_of,), jnp.float32, least / len(shards), high / len(shards))
        return jnp.repeat(jnp.exp(heights), shape[position] // shards_of).reshape((-1,) + (1,) * (len(shape) - position - 1))

    level = one(*shards[0])
    for cut in shards[1:]:
        level = level * one(*cut)
    return level


def normal_values(stream_key, extent, width, limit, cuts=(), dtype=jnp.bfloat16):
    values = width * jax.random.normal(stream_key, extent, jnp.float32)
    if cuts:
        values = values * levels(stream_key, extent, cuts, -0.22, 0.18)
    return jnp.clip(values, -limit, limit).astype(dtype)


def setup_inputs(seed: int = 0) -> dict:
    splits = jax.random.split(jax.random.key(seed), 9)
    return {
        "entering": normal_values(splits[0], (M, L, D), 1.0, 6.0, ((1, 32),)),
        "in_store": normal_values(splits[1], (N_PIPE, M, L, D), 1.0, 6.0, ((0, 4), (2, 32))),
        "out_store": normal_values(splits[2], (N_PIPE, M, L, D), 1.0, 6.0, ((0, 4), (2, 32))),
        "norm_gain": jnp.clip(1.0 + 0.15 * jax.random.normal(splits[3], (N_PIPE, D), jnp.float32), 0.25, 1.75).astype(jnp.bfloat16),
        "adapter_down": normal_values(splits[4], (N_PIPE, D, R), D ** -0.5, 0.0625, ((0, 4), (1, 32))),
        "adapter_up": normal_values(splits[5], (N_PIPE, R, D), R ** -0.5, 0.375, ((0, 4), (2, 32))),
        "sample_ids": jax.random.permutation(splits[6], M).astype(jnp.int32),
        "cotangent": normal_values(splits[7], (M, L, D), 1.0, 6.0, ((1, 32),)),
    }


def section_forward(section_in, gain_vec, down_mat, up_mat):
    values = section_in.astype(jnp.float32)
    inv_rms = lax.rsqrt(lax.optimization_barrier(jnp.mean(values * values, axis=-1, keepdims=True)) + 1e-05)
    normed = (values * inv_rms * gain_vec.astype(jnp.float32)).astype(jnp.bfloat16)
    hidden = jax.nn.silu(jnp.dot(normed, down_mat, preferred_element_type=jnp.float32)).astype(jnp.bfloat16)
    return values + jnp.dot(hidden, up_mat, preferred_element_type=jnp.float32)

def encode_rows(value):
    row_scale = lax.optimization_barrier(jnp.max(jnp.abs(value), axis=-1)) + 1e-06
    packed = (value / row_scale[:, None]).astype(jnp.bfloat16)
    return (packed, row_scale)

def backward_core(section_in, grad_out, gain_vec, down_mat, up_mat):
    values = section_in.astype(jnp.float32)
    inv_rms = lax.rsqrt(lax.optimization_barrier(jnp.mean(values * values, axis=-1, keepdims=True)) + 1e-05)
    gain_f = gain_vec.astype(jnp.float32)
    unit = values * inv_rms
    normed = (unit * gain_f).astype(jnp.bfloat16)
    pre_act = jnp.dot(normed, down_mat, preferred_element_type=jnp.float32)
    hidden = jax.nn.silu(pre_act).astype(jnp.bfloat16)
    grad_bf = grad_out.astype(jnp.bfloat16)
    grad_hidden = lax.dot_general(grad_bf, up_mat, (((1,), (1,)), ((), ())), preferred_element_type=jnp.float32)
    sigma = jax.nn.sigmoid(pre_act)
    grad_pre = (grad_hidden * sigma * (1.0 + pre_act * (1.0 - sigma))).astype(jnp.bfloat16)
    grad_normed = lax.dot_general(grad_pre, down_mat, (((1,), (1,)), ((), ())), preferred_element_type=jnp.float32)
    gain_terms = grad_normed * unit
    grad_unit = grad_normed * gain_f
    grad_in = grad_out + inv_rms * (grad_unit - unit * lax.optimization_barrier(jnp.mean(grad_unit * unit, axis=-1, keepdims=True)))
    return (grad_in, normed, hidden, grad_bf, grad_pre, gain_terms)

def reference(entering, in_store, out_store, norm_gain, adapter_down, adapter_up, sample_ids, cotangent):
    section_count = in_store.shape[0]
    micro_count = entering.shape[0]
    inputs_rows = [[None] * micro_count for _ in range(section_count)]
    sent_rows = [[None] * micro_count for _ in range(section_count)]
    for micro_pos in range(micro_count):
        sample_row = sample_ids[micro_pos]
        current = (in_store[0, sample_row].astype(jnp.float32) + entering[micro_pos].astype(jnp.float32)).astype(jnp.bfloat16)
        for section_pos in range(section_count):
            inputs_rows[section_pos][micro_pos] = current
            result = section_forward(current, norm_gain[section_pos], adapter_down[section_pos], adapter_up[section_pos])
            previous = out_store[section_pos, sample_row].astype(jnp.float32)
            packed, row_scale = encode_rows(result - previous)
            decoded = row_scale[:, None] * packed.astype(jnp.float32)
            sent_rows[section_pos][micro_pos] = (previous + decoded).astype(jnp.bfloat16)
            if section_pos + 1 < section_count:
                current = (in_store[section_pos + 1, sample_row].astype(jnp.float32) + decoded).astype(jnp.bfloat16)
    grads_rows = [[None] * micro_count for _ in range(section_count)]
    acc_gain = [jnp.zeros((N_FSDP, D), jnp.float32) for _ in range(section_count)]
    acc_down = [jnp.zeros((N_FSDP, D, R), jnp.float32) for _ in range(section_count)]
    acc_up = [jnp.zeros((N_FSDP, R, D), jnp.float32) for _ in range(section_count)]
    for micro_pos in range(micro_count):
        grad_out = cotangent[micro_pos].astype(jnp.float32)
        for section_pos in range(section_count - 1, -1, -1):
            grad_in, normed, hidden, grad_bf, grad_pre, gain_terms = backward_core(inputs_rows[section_pos][micro_pos], grad_out, norm_gain[section_pos], adapter_down[section_pos], adapter_up[section_pos])
            grads_rows[section_pos][micro_pos] = grad_in.astype(jnp.bfloat16)
            normed_b = normed.astype(jnp.float32).reshape(N_FSDP, -1, D)
            pre_b = grad_pre.astype(jnp.float32).reshape(N_FSDP, -1, R)
            hidden_b = hidden.astype(jnp.float32).reshape(N_FSDP, -1, R)
            grad_b = grad_bf.astype(jnp.float32).reshape(N_FSDP, -1, D)
            acc_down[section_pos] = acc_down[section_pos] + jnp.einsum('frd,frk->fdk', normed_b, pre_b)
            acc_up[section_pos] = acc_up[section_pos] + jnp.einsum('frk,frd->fkd', hidden_b, grad_b)
            acc_gain[section_pos] = acc_gain[section_pos] + lax.optimization_barrier(jnp.sum(gain_terms.reshape(N_FSDP, -1, D), axis=1))
            packed, row_scale = encode_rows(grad_in)
            grad_out = row_scale[:, None] * packed.astype(jnp.float32)

    def block_total(parts):
        rounded = lax.optimization_barrier(parts.astype(jnp.bfloat16))
        return lax.optimization_barrier(jnp.sum(rounded.astype(jnp.float32), axis=0))
    sent_refresh = jnp.stack([jnp.stack(row) for row in sent_rows])
    section_inputs = jnp.stack([jnp.stack(row) for row in inputs_rows])
    input_grads = jnp.stack([jnp.stack(row) for row in grads_rows])
    grad_gain = jnp.stack([block_total(part) for part in acc_gain])
    grad_down = jnp.stack([block_total(part) for part in acc_down])
    grad_up = jnp.stack([block_total(part) for part in acc_up])
    return (sent_refresh, section_inputs, input_grads, grad_gain, grad_down, grad_up)
```

```python
import jax
import jax.numpy as jnp
from jax import lax
from jax.experimental import pallas as pl
from jax.experimental.pallas import tpu as pltpu
from jax.sharding import PartitionSpec as P

EPS = 1e-05
TINY = 1e-06
NZ, NX, NY = 2, 4, 4
NF = NZ * NX * NY
BLK = 256
PAD = 16
CODE = 128
F32 = jnp.float32
BF = jnp.bfloat16
VMEM_LIMIT = 56 * 1024 * 1024


def flat(z, x, y):
    return (z % NZ) * (NX * NY) + (x % NX) * NY + (y % NY)


def shift(block, dz, dx, dy):
    route = [
        (flat(z, x, y), flat(z + dz, x + dx, y + dy))
        for z in range(NZ)
        for x in range(NX)
        for y in range(NY)
    ]
    return lax.ppermute(block, "fsdp", route)


def any_spec():
    return pl.BlockSpec(memory_space=pl.ANY)


def smem_spec():
    return pl.BlockSpec(memory_space=pltpu.SMEM)


def cols(index):
    return pl.ds(pl.multiple_of(index * BLK, BLK), BLK)


NCH = 4
PER = NF // NCH


def start_weights(src, dst, sems, base):
    copies = []
    for c in range(NCH):
        copy = pltpu.make_async_copy(
            src.at[pl.ds(c * PER, PER)], dst.at[pl.ds(c * PER, PER)], sems.at[base + c]
        )
        copy.start()
        copies.append(copy)
    return copies


def forward_kernel(
    s_ref, fa, fb, ent, ins, outs, arr, wd, wu, _ib, _sb, _pb, _vb,
    ib, sb, pb, vb, pk,
    arr_v, in_v, out_v, wd_v, wu_v, x_v, v_v, ref_v, pk_v, pre_v, inv_v, sems,
):
    width = in_v.shape[1]
    live, m, j, first = s_ref[0], s_ref[1], s_ref[2], s_ref[3]

    @pl.when(live == 1)
    def _():
        cp_in = pltpu.make_async_copy(ins.at[j], in_v, sems.at[0])
        cp_in.start()

        @pl.when(first == 1)
        def _():
            cp = pltpu.make_async_copy(ent.at[m], arr_v.at[:, pl.ds(0, width)], sems.at[1])
            cp.start()
            cp.wait()
            arr_v[:, width:] = jnp.ones((arr_v.shape[0], CODE), BF)

        @pl.when(first == 0)
        def _():
            cp = pltpu.make_async_copy(arr, arr_v, sems.at[1])
            cp.start()
            cp.wait()

        wd_copies = start_weights(wd, wd_v, sems, 8)
        cp_out = pltpu.make_async_copy(outs.at[j], out_v, sems.at[2])
        cp_out.start()
        wu_copies = start_weights(wu, wu_v, sems, 8 + NCH)
        cp_in.wait()

        scale_in = arr_v[:, pl.ds(width, 1)].astype(F32)

        def enter(i, acc):
            c = cols(i)
            x = (in_v[:, c].astype(F32) + scale_in * arr_v[:, c].astype(F32)).astype(BF)
            x_v[:, c] = x
            xf = x.astype(F32)
            return acc + xf * xf

        zero = jnp.zeros((x_v.shape[0], BLK), F32)
        square = lax.fori_loop(0, NF, enter, zero, unroll=4)
        cp_x = pltpu.make_async_copy(x_v, ib.at[m], sems.at[3])
        cp_x.start()
        inv = lax.rsqrt(jnp.sum(square, axis=-1, keepdims=True) * (1.0 / width) + EPS)
        inv_v[...] = jnp.broadcast_to(inv, inv_v.shape)

        pre = zero
        for k in range(NF):
            if k % PER == 0:
                wd_copies[k // PER].wait()
            gain = wd_v[k, pl.ds(BLK, PAD), :][0:1].astype(F32)
            normed = (x_v[:, cols(fa[k])].astype(F32) * inv * gain).astype(BF)
            pre = pre + jnp.dot(normed, wd_v[k, pl.ds(0, BLK), :], preferred_element_type=F32)
        pre_v[...] = pre
        hidden = (pre * jax.nn.sigmoid(pre)).astype(BF)
        cp_pre = pltpu.make_async_copy(pre_v, pb.at[m], sems.at[4])
        cp_pre.start()
        cp_inv = pltpu.make_async_copy(inv_v, vb.at[m], sems.at[5])
        cp_inv.start()

        cp_out.wait()
        top = zero
        for k in range(NF):
            if k % PER == 0:
                wu_copies[k // PER].wait()
            c = cols(fb[k])
            v = (
                x_v[:, c].astype(F32)
                + jnp.dot(hidden, wu_v[k], preferred_element_type=F32)
                - out_v[:, c].astype(F32)
            )
            v_v[:, c] = v
            top = jnp.maximum(top, jnp.abs(v))
        scale_b = (jnp.max(top, axis=-1, keepdims=True) + TINY).astype(BF)
        scale = scale_b.astype(F32)
        inverse = 1.0 / scale
        pk_v[:, pl.ds(width, CODE)] = jnp.broadcast_to(scale_b, (pk_v.shape[0], CODE))

        def code(i, carry):
            c = cols(i)
            packed = (v_v[:, c] * inverse).astype(BF)
            pk_v[:, c] = packed
            ref_v[:, c] = (out_v[:, c].astype(F32) + scale * packed.astype(F32)).astype(BF)
            return carry

        lax.fori_loop(0, NF, code, 0, unroll=4)
        cp_pk = pltpu.make_async_copy(pk_v, pk, sems.at[6])
        cp_pk.start()
        cp_ref = pltpu.make_async_copy(ref_v, sb.at[m], sems.at[7])
        cp_ref.start()
        cp_x.wait()
        cp_pre.wait()
        cp_inv.wait()
        cp_pk.wait()
        cp_ref.wait()


def backward_kernel(
    s_ref, fa, fb, cot, arr, wd, wu, _ib, _pb, _vb, _gb, _xb, _qb, _nb,
    ib, pb, vb, gb, xb, qb, nb, pk,
    arr_v, x_v, wd_v, wu_v, g_v, u_v, dx_v, pk_v, pre_v, inv_v, gp_v, gn_v, sems,
):
    rows, width = x_v.shape
    live, m, first = s_ref[0], s_ref[1], s_ref[2]

    @pl.when(live == 1)
    def _():
        cp_x = pltpu.make_async_copy(ib.at[m], x_v, sems.at[0])
        cp_pre = pltpu.make_async_copy(pb.at[m], pre_v, sems.at[2])
        cp_inv = pltpu.make_async_copy(vb.at[m], inv_v, sems.at[3])

        @pl.when(first == 1)
        def _():
            cp = pltpu.make_async_copy(cot.at[m], arr_v.at[:, pl.ds(0, width)], sems.at[1])
            cp.start()
            cp.wait()
            arr_v[:, width:] = jnp.ones((rows, CODE), BF)

        @pl.when(first == 0)
        def _():
            cp = pltpu.make_async_copy(arr, arr_v, sems.at[1])
            cp.start()
            cp.wait()

        wu_copies = start_weights(wu, wu_v, sems, 8)
        cp_pre.start()
        cp_inv.start()
        cp_x.start()
        wd_copies = start_weights(wd, wd_v, sems, 8 + NCH)
        scale_in = arr_v[:, pl.ds(width, 1)].astype(F32)

        zero = jnp.zeros((rows, BLK), F32)
        gh = zero
        for k in range(NF):
            if k % PER == 0:
                wu_copies[k // PER].wait()
            c = cols(fb[k])
            g = (scale_in * arr_v[:, c].astype(F32)).astype(BF)
            g_v[:, c] = g
            gh = gh + lax.dot_general(
                g, wu_v[k], (((1,), (1,)), ((), ())), preferred_element_type=F32
            )
        cp_g = pltpu.make_async_copy(g_v, gb.at[m], sems.at[4])
        cp_g.start()
        cp_pre.wait()
        cp_inv.wait()
        pre = pre_v[...]
        inv = inv_v[:, pl.ds(0, 1)]
        sigma = jax.nn.sigmoid(pre)
        gp = (gh * sigma * (1.0 + pre * (1.0 - sigma))).astype(BF)
        gp_v[...] = gp
        cp_gp = pltpu.make_async_copy(gp_v, qb.at[m], sems.at[5])
        cp_gp.start()
        cp_x.wait()
        dots = zero
        for k in range(NF):
            if k % PER == 0:
                wd_copies[k // PER].wait()
            c = cols(fa[k])
            gain = wd_v[k, pl.ds(BLK, PAD), :][0:1].astype(F32)
            gn = lax.dot_general(
                gp, wd_v[k, pl.ds(0, BLK), :], (((1,), (1,)), ((), ())), preferred_element_type=F32
            )
            unit = x_v[:, c].astype(F32) * inv
            term = gn * unit
            gn_v[:, c] = jnp.sum(term.reshape(rows // 8, 8, BLK), axis=0)
            gu = gn * gain
            u_v[:, c] = gu
            dots = dots + gu * unit
        cp_gn = pltpu.make_async_copy(gn_v, nb.at[m], sems.at[6])
        cp_gn.start()
        mean = jnp.sum(dots, axis=-1, keepdims=True) * (1.0 / width)

        def leave(i, top):
            c = cols(i)
            dx = scale_in * arr_v[:, c].astype(F32) + inv * (
                u_v[:, c] - x_v[:, c].astype(F32) * inv * mean
            )
            u_v[:, c] = dx
            dx_v[:, c] = dx.astype(BF)
            return jnp.maximum(top, jnp.abs(dx))

        top = lax.fori_loop(0, NF, leave, zero, unroll=4)
        cp_dx = pltpu.make_async_copy(dx_v, xb.at[m], sems.at[7])
        cp_dx.start()
        scale_b = (jnp.max(top, axis=-1, keepdims=True) + TINY).astype(BF)
        inverse = 1.0 / scale_b.astype(F32)
        pk_v[:, pl.ds(width, CODE)] = jnp.broadcast_to(scale_b, (rows, CODE))

        def code(i, carry):
            c = cols(i)
            pk_v[:, c] = (u_v[:, c] * inverse).astype(BF)
            return carry

        lax.fori_loop(0, NF, code, 0, unroll=4)
        cp_pk = pltpu.make_async_copy(pk_v, pk, sems.at[0])
        cp_pk.start()
        cp_g.wait()
        cp_gp.wait()
        cp_gn.wait()
        cp_dx.wait()
        cp_pk.wait()


ORDER = (2, 1, 3, 0)


def partial_kernel(
    pos, x_hbm, g_hbm, pre_hbm, inv_hbm, gp_hbm, gn_hbm, gain_hbm,
    a2, a1, a3, a0, b2, b1, b3, b0,
    x_v, g_v, pre_v, inv_v, gp_v, gn_v, gain_v, ht_v, gt_v, out_a, out_b, sems, osems,
):
    loads = []
    for i, (src, dst) in enumerate(
        ((pre_hbm, pre_v), (gp_hbm, gp_v), (inv_hbm, inv_v), (gn_hbm, gn_v), (gain_hbm, gain_v),
         (x_hbm, x_v), (g_hbm, g_v))
    ):
        cp = pltpu.make_async_copy(src, dst, sems.at[i])
        cp.start()
        loads.append(cp)
    z, x, y = pos[0], pos[1], pos[2]
    loads[0].wait()
    loads[1].wait()
    pre = pre_v[...]
    ht_v[...] = (pre * jax.nn.sigmoid(pre)).T.astype(BF)
    gt_v[...] = gp_v[...].astype(F32).T.astype(BF)
    for cp in loads[2:]:
        cp.wait()
    inv = inv_v[:, pl.ds(0, 1)]
    stores = []
    for n, (step, a_out, b_out) in enumerate(zip(ORDER, (a2, a1, a3, a0), (b2, b1, b3, b0))):
        for e in range(8):
            other, kz = e // 2, e % 2
            zz = lax.rem(z + kz, NZ) * (NX * NY)
            c = cols(zz + lax.rem(x + other, NX) * NY + lax.rem(y + step, NY))
            normed = (x_v[:, c].astype(F32) * inv * gain_v[pl.ds(0, 1), c]).astype(BF)
            out_a[n, e, pl.ds(0, BLK), :] = jnp.dot(
                gt_v[...], normed, preferred_element_type=F32
            ).astype(BF)
            row = jnp.sum(gn_v[0, :, c] + gn_v[1, :, c] + gn_v[2, :, c], axis=0, keepdims=True)
            out_a[n, e, pl.ds(BLK, PAD), :] = jnp.broadcast_to(row, (PAD, BLK)).astype(BF)
            c = cols(zz + lax.rem(x + step, NX) * NY + lax.rem(y + other, NY))
            out_b[n, e] = jnp.dot(ht_v[...], g_v[:, c], preferred_element_type=F32).astype(BF)
        cp = pltpu.make_async_copy(out_a.at[n], a_out, osems.at[2 * n])
        cp.start()
        stores.append(cp)
        cp = pltpu.make_async_copy(out_b.at[n], b_out, osems.at[2 * n + 1])
        cp.start()
        stores.append(cp)
    for cp in stores:
        cp.wait()


def gather_weights(down, up, gain):
    own_a = jnp.concatenate([down, jnp.broadcast_to(gain, (PAD, BLK))], axis=0)
    z_a = shift(own_a, 1, 0, 0)
    z_b = shift(up, 1, 0, 0)

    def two_axes(pair, first, second):
        one = [pair] + [shift(pair, *first(-d)) for d in (1, 3, 2)]
        pieces = []
        for label, piece in (((0,), pair), ((1, 3, 2), jnp.concatenate(one[1:], axis=0))):
            half = piece.shape[0] // 2
            ahead = shift(piece, *second(-1))
            behind = shift(piece, *second(1))
            far_lo = shift(ahead[:half], *second(-1))
            far_hi = shift(behind[half:], *second(1))
            keys = [(d, kz) for d in label for kz in range(NZ)]
            pieces += [
                ([(d, 0, kz) for d, kz in keys], piece),
                ([(d, 1, kz) for d, kz in keys], ahead),
                ([(d, 3, kz) for d, kz in keys], behind),
                ([(d, 2, kz) for d, kz in keys[:half]], far_lo),
                ([(d, 2, kz) for d, kz in keys[half:]], far_hi),
            ]
        keys = [key for part, _ in pieces for key in part]
        return keys, jnp.concatenate([piece for _, piece in pieces], axis=0)

    along_x = lambda d: (0, d, 0)
    along_y = lambda d: (0, 0, d)
    keys_a, blocks_a = two_axes(jnp.stack([own_a, z_a]), along_x, along_y)
    keys_b, blocks_b = two_axes(jnp.stack([up, z_b]), along_y, along_x)
    keys_a = [(kz, d, e) for d, e, kz in keys_a]
    keys_b = [(kz, e, d) for d, e, kz in keys_b]
    return keys_a, blocks_a, keys_b, blocks_b


def place(keys, z, x, y):
    keys = jnp.array(keys, jnp.int32)
    return (
        lax.rem(z + keys[:, 0], NZ) * (NX * NY)
        + lax.rem(x + keys[:, 1], NX) * NY
        + lax.rem(y + keys[:, 2], NY)
    ).astype(jnp.int32)


def add_up(*terms):
    return sum(t.astype(F32) for t in terms).astype(BF)


def scatter_two(groups, first, second):
    g0, g1, g2, g3 = groups
    half = g0.shape[0] // 2
    far_lo = shift(g2[:half], *first(1))
    far_hi = shift(g2[half:], *first(-1))
    up_hi = shift(g1[half:], *first(1))
    down_lo = shift(g3[:half], *first(-1))
    up_lo = shift(add_up(g1[:half], far_lo), *first(1))
    down_hi = shift(add_up(g3[half:], far_hi), *first(-1))
    lo = add_up(g0[:half], up_lo, down_lo)
    hi = add_up(g0[half:], up_hi, down_hi)
    ahead = shift(lo[2:4], *second(1))
    far = shift(hi[0:2], *second(2))
    behind = shift(hi[2:4], *second(-1))
    return add_up(lo[0:2], ahead, far, behind)


def per_device(entering, in_store, out_store, norm_gain, adapter_down, adapter_up, sample_ids, cotangent):
    n_sec = lax.axis_size("pipe")
    sec = lax.axis_index("pipe")
    f = lax.axis_index("fsdp")
    z, x, y = f // (NX * NY), lax.rem(f // NY, NX), lax.rem(f, NY)
    n_micro, rows, width = entering.shape
    r = adapter_up.shape[1]

    keys_a, wd, keys_b, wu = gather_weights(adapter_down[0], adapter_up[0], norm_gain)
    fa, fb = place(keys_a, z, x, y), place(keys_b, z, x, y)

    big = jax.ShapeDtypeStruct((n_micro, rows, width), BF)
    pre_t = jax.ShapeDtypeStruct((n_micro, rows, r), F32)
    inv_t = jax.ShapeDtypeStruct((n_micro, rows, 128), F32)
    gp_t = jax.ShapeDtypeStruct((n_micro, rows, r), BF)
    gn_t = jax.ShapeDtypeStruct((n_micro, 8, width), F32)
    pk_t = jax.ShapeDtypeStruct((rows, width + CODE), BF)
    params = pltpu.CompilerParams(vmem_limit_bytes=VMEM_LIMIT)

    def zeros(t):
        return jnp.zeros(t.shape, t.dtype)

    wide = pltpu.VMEM((rows, width), BF)
    wide_f = pltpu.VMEM((rows, width), F32)
    coded = pltpu.VMEM((rows, width + CODE), BF)
    weights = [pltpu.VMEM(wd.shape, BF), pltpu.VMEM(wu.shape, BF)]
    small = [pltpu.VMEM((rows, r), F32), pltpu.VMEM((rows, 128), F32)]
    sems = pltpu.SemaphoreType.DMA((8 + 2 * NCH,))

    def forward(scalars, arrived, ib, sb, pb, vb):
        return pl.pallas_call(
            forward_kernel,
            out_shape=(big, big, pre_t, inv_t, pk_t),
            in_specs=[smem_spec()] * 3 + [any_spec()] * 10,
            out_specs=[any_spec()] * 5,
            scratch_shapes=[coded, wide, wide] + weights + [wide, wide_f, wide, coded] + small + [sems],
            input_output_aliases={9: 0, 10: 1, 11: 2, 12: 3},
            compiler_params=params,
            cost_estimate=pl.CostEstimate(
                flops=4 * rows * width * r, bytes_accessed=16 * 1024 * 1024, transcendentals=0
            ),
            name="section_forward",
        )(scalars, fa, fb, entering, in_store[0], out_store[0], arrived, wd, wu, ib, sb, pb, vb)

    def backward(scalars, arrived, ib, pb, vb, gb, xb, qb, nb):
        return pl.pallas_call(
            backward_kernel,
            out_shape=(big, pre_t, inv_t, big, big, gp_t, gn_t, pk_t),
            in_specs=[smem_spec()] * 3 + [any_spec()] * 11,
            out_specs=[any_spec()] * 8,
            scratch_shapes=[coded, wide] + weights + [wide, wide_f, wide, coded] + small
            + [pltpu.VMEM((rows, r), BF), pltpu.VMEM((8, width), F32), sems],
            input_output_aliases={7: 0, 8: 1, 9: 2, 10: 3, 11: 4, 12: 5, 13: 6},
            compiler_params=params,
            cost_estimate=pl.CostEstimate(
                flops=4 * rows * width * r, bytes_accessed=16 * 1024 * 1024, transcendentals=0
            ),
            name="section_backward",
        )(scalars, fa, fb, cotangent, arrived, wd, wu, ib, pb, vb, gb, xb, qb, nb)

    ib, sb, gb, xb = zeros(big), zeros(big), zeros(big), zeros(big)
    pb, vb, qb, nb = zeros(pre_t), zeros(inv_t), zeros(gp_t), zeros(gn_t)
    arrived, returned = zeros(pk_t), zeros(pk_t)
    last = n_micro + 2 * (n_sec - 1)
    for tick in range(last):
        sent = back = None
        if tick < n_micro + n_sec - 1:
            m = tick - sec
            live = (m >= 0) & (m < n_micro)
            slot = jnp.clip(m, 0, n_micro - 1)
            scalars = jnp.stack([live, slot, sample_ids[slot], sec == 0]).astype(jnp.int32)
            ib, sb, pb, vb, sent = forward(scalars, arrived, ib, sb, pb, vb)
            edges = [(s, s + 1) for s in range(n_sec - 1) if 0 <= tick - s < n_micro]
            arrived = lax.ppermute(sent, "pipe", edges) if edges else arrived
        if tick >= n_sec - 1:
            m = tick - 2 * (n_sec - 1) + sec
            live = (m >= 0) & (m < n_micro)
            slot = jnp.clip(m, 0, n_micro - 1)
            scalars = jnp.stack([live, slot, sec == n_sec - 1]).astype(jnp.int32)
            ib, pb, vb, gb, xb, qb, nb, back = backward(scalars, returned, ib, pb, vb, gb, xb, qb, nb)
            edges = [
                (s, s - 1) for s in range(1, n_sec) if 0 <= tick - 2 * (n_sec - 1) + s < n_micro
            ]
            returned = lax.ppermute(back, "pipe", edges) if edges else returned

    gain_full = jnp.zeros((NF, BLK), F32).at[fa].set(wd[:, BLK, :].astype(F32)).reshape(1, width)
    gain_full = jnp.broadcast_to(gain_full, (8, width))
    all_rows = n_micro * rows
    group_a = jax.ShapeDtypeStruct((8, BLK + PAD, BLK), BF)
    group_b = jax.ShapeDtypeStruct((8, r, BLK), BF)
    a2, a1, a3, a0, b2, b1, b3, b0 = pl.pallas_call(
        partial_kernel,
        out_shape=(group_a,) * 4 + (group_b,) * 4,
        in_specs=[smem_spec()] + [any_spec()] * 7,
        out_specs=[any_spec()] * 8,
        scratch_shapes=[
            pltpu.VMEM((all_rows, width), BF),
            pltpu.VMEM((all_rows, width), BF),
            pltpu.VMEM((all_rows, r), F32),
            pltpu.VMEM((all_rows, 128), F32),
            pltpu.VMEM((all_rows, r), BF),
            pltpu.VMEM((n_micro, 8, width), F32),
            pltpu.VMEM((8, width), F32),
            pltpu.VMEM((r, all_rows), BF),
            pltpu.VMEM((r, all_rows), BF),
            pltpu.VMEM((4, 8, BLK + PAD, BLK), BF),
            pltpu.VMEM((4, 8, r, BLK), BF),
            pltpu.SemaphoreType.DMA((7,)),
            pltpu.SemaphoreType.DMA((8,)),
        ],
        compiler_params=params,
        name="gradient_partials",
    )(
        jnp.stack([z, x, y]).astype(jnp.int32),
        ib.reshape(all_rows, width), gb.reshape(all_rows, width), pb.reshape(all_rows, r),
        vb.reshape(all_rows, 128), qb.reshape(all_rows, r), nb, gain_full,
    )
    along_x = lambda d: (0, d, 0)
    along_y = lambda d: (0, 0, d)
    sum_a = scatter_two((a0, a1, a2, a3), along_y, along_x)
    sum_b = scatter_two((b0, b1, b2, b3), along_x, along_y)
    total_a = sum_a[0].astype(F32) + shift(sum_a[1], 1, 0, 0).astype(F32)
    total_b = sum_b[0].astype(F32) + shift(sum_b[1], 1, 0, 0).astype(F32)
    return (
        sb[None],
        ib[None],
        xb[None],
        total_a[BLK : BLK + 1],
        total_a[:BLK].T[None],
        total_b[None],
    )


def solution(mesh):
    return jax.shard_map(
        per_device,
        mesh=mesh,
        in_specs=(
            P(None, "fsdp", None),
            P("pipe", None, "fsdp", None),
            P("pipe", None, "fsdp", None),
            P("pipe", "fsdp"),
            P("pipe", "fsdp", None),
            P("pipe", None, "fsdp"),
            P(),
            P(None, "fsdp", None),
        ),
        out_specs=(
            P("pipe", None, "fsdp", None),
            P("pipe", None, "fsdp", None),
            P("pipe", None, "fsdp", None),
            P("pipe", "fsdp"),
            P("pipe", "fsdp", None),
            P("pipe", None, "fsdp"),
        ),
        check_vma=False,
    )
```

```python
import jax
import jax.numpy as jnp
from jax import lax
from jax.experimental import pallas as pl
from jax.experimental.pallas import tpu as pltpu
from jax.sharding import PartitionSpec as P

EPS = 1e-05
TINY = 1e-06
NZ, NX, NY = 2, 4, 4
NF = NZ * NX * NY
BLK = 256
CODE = 128
F32 = jnp.float32
BF = jnp.bfloat16
VMEM_LIMIT = 20 * 1024 * 1024


def flat(z, x, y):
    return (z % NZ) * (NX * NY) + (x % NX) * NY + (y % NY)


def shift(block, dz, dx, dy):
    route = [
        (flat(z, x, y), flat(z + dz, x + dx, y + dy))
        for z in range(NZ)
        for x in range(NX)
        for y in range(NY)
    ]
    return lax.ppermute(block, "fsdp", route)


def any_spec():
    return pl.BlockSpec(memory_space=pl.ANY)


def hbm_spec():
    return pl.BlockSpec(memory_space=pltpu.HBM)


def smem_spec():
    return pl.BlockSpec(memory_space=pltpu.SMEM)


def cols(index):
    return pl.ds(pl.multiple_of(index * BLK, BLK), BLK)


PIECES = 8
PER = NF // PIECES


def weight_spec():
    return pl.BlockSpec(memory_space=pltpu.VMEM)


def fetch(uncoded, arrivals, dst, sem, source):
    rows, width = uncoded.shape
    copies = [pltpu.make_async_copy(uncoded, dst.at[:, pl.ds(0, width)], sem)]
    copies += [pltpu.make_async_copy(arrival, dst, sem) for arrival in arrivals]
    for i, copy in enumerate(copies):
        pl.when(source == i)(copy.start)

    def wait():
        for i, copy in enumerate(copies):
            pl.when(source == i)(copy.wait)

        @pl.when(source == 0)
        def _():
            dst[:, width:] = jnp.ones((rows, CODE), BF)

    return wait


def forward_kernel(tick, fresh, *refs):
    at = 6 if fresh else 8
    s_ref, fa, fb, ent, ins, outs = refs[:6]
    if fresh:
        n_in = at + 2 * PIECES
        pieces, (wd, wu) = refs[at:n_in], refs[n_in + 5 : n_in + 7]
        ib, sb, pb, vb, pk = refs[n_in : n_in + 5]
        scratch = refs[n_in + 7 :]
    else:
        wd, wu = refs[at : at + 2]
        n_in = at + 2 + 4
        ib, sb, pb, vb, pk = refs[n_in : n_in + 5]
        scratch = refs[n_in + 5 :]
    arr_v, in_v, out_v, x_v, v_v, ref_v, pk_v, pre_v, inv_v, sems = scratch
    rows, width = in_v.shape
    live, m, j, source = s_ref[tick, 0], s_ref[tick, 1], s_ref[tick, 2], s_ref[tick, 3]
    loads = []
    if fresh:
        for i, piece in enumerate(pieces):
            whole = (wd, wu)[i // PIECES].at[pl.ds(i % PIECES * PER, PER)]
            loads.append(pltpu.make_async_copy(piece, whole, sems.at[8 + i]))

    @pl.when(live == 1)
    def _():
        cp_in = pltpu.make_async_copy(ins.at[j], in_v, sems.at[0])
        cp_in.start()
        await_arrival = fetch(ent.at[m], refs[6:at], arr_v, sems.at[1], source)
        for load in loads[:PIECES]:
            load.start()
        cp_out = pltpu.make_async_copy(outs.at[j], out_v, sems.at[2])
        cp_out.start()
        for load in loads[PIECES:]:
            load.start()

        await_arrival()
        cp_in.wait()

        scale_in = arr_v[:, pl.ds(width, 1)].astype(F32)
        zero = jnp.zeros((rows, BLK), F32)
        square = pre = zero
        for k in range(NF):
            if fresh and k % PER == 0:
                loads[k // PER].wait()
            c = cols(fa[k])
            x = (in_v[:, c].astype(F32) + scale_in * arr_v[:, c].astype(F32)).astype(BF)
            x_v[:, c] = x
            xf = x.astype(F32)
            square = square + xf * xf
            pre = pre + jnp.dot(x, wd[k], preferred_element_type=F32)
        cp_x = pltpu.make_async_copy(x_v, ib.at[m], sems.at[3])
        cp_x.start()
        inv = lax.rsqrt(jnp.sum(square, axis=-1, keepdims=True) * (1.0 / width) + EPS)
        inv_v[...] = jnp.broadcast_to(inv, inv_v.shape)
        pre = pre * inv
        pre_v[...] = pre
        hidden = (pre * jax.nn.sigmoid(pre)).astype(BF)
        cp_pre = pltpu.make_async_copy(pre_v, pb.at[m], sems.at[4])
        cp_pre.start()
        cp_inv = pltpu.make_async_copy(inv_v, vb.at[m], sems.at[5])
        cp_inv.start()

        cp_out.wait()
        top = zero
        for k in range(NF):
            if fresh and k % PER == 0:
                loads[PIECES + k // PER].wait()
            c = cols(fb[k])
            v = (
                x_v[:, c].astype(F32)
                + jnp.dot(hidden, wu[k], preferred_element_type=F32)
                - out_v[:, c].astype(F32)
            )
            v_v[:, c] = v
            top = jnp.maximum(top, jnp.abs(v))
        scale_b = (jnp.max(top, axis=-1, keepdims=True) + TINY).astype(BF)
        scale = scale_b.astype(F32)
        inverse = 1.0 / scale
        pk_v[:, pl.ds(width, CODE)] = jnp.broadcast_to(scale_b, (rows, CODE))

        def code(i, carry):
            c = cols(i)
            packed = (v_v[:, c] * inverse).astype(BF)
            pk_v[:, c] = packed
            ref_v[:, c] = (out_v[:, c].astype(F32) + scale * packed.astype(F32)).astype(BF)
            return carry

        lax.fori_loop(0, NF, code, 0, unroll=4)
        cp_pk = pltpu.make_async_copy(pk_v, pk, sems.at[6])
        cp_pk.start()
        cp_ref = pltpu.make_async_copy(ref_v, sb.at[m], sems.at[7])
        cp_ref.start()
        cp_x.wait()
        cp_pre.wait()
        cp_inv.wait()
        cp_pk.wait()
        cp_ref.wait()

    if fresh:

        @pl.when(live == 0)
        def _():
            for load in loads:
                load.start()
            for load in loads:
                load.wait()


def backward_kernel(tick, fresh, *refs):
    at = 4 if fresh else 6
    s_ref, fa, fb, cot = refs[:4]
    wd, wu = refs[at : at + 2]
    n_in = at + 2 + 3 + (0 if fresh else 4)
    ib, pb, vb, gb, xb, hb, qb, pk = refs[n_in : n_in + 8]
    arr_v, x_v, u_v, dx_v, pk_v, pre_v, inv_v, hs_v, gs_v, sems = refs[n_in + 8 :]
    rows, width = x_v.shape
    live, m, source = s_ref[tick, 4], s_ref[tick, 5], s_ref[tick, 6]

    @pl.when(live == 1)
    def _():
        await_arrival = fetch(cot.at[m], refs[4:at], arr_v, sems.at[1], source)
        cp_x = pltpu.make_async_copy(ib.at[m], x_v, sems.at[0])
        cp_pre = pltpu.make_async_copy(pb.at[m], pre_v, sems.at[2])
        cp_inv = pltpu.make_async_copy(vb.at[m], inv_v, sems.at[3])
        cp_pre.start()
        cp_inv.start()
        cp_x.start()
        await_arrival()
        cp_g = pltpu.make_async_copy(arr_v.at[:, pl.ds(0, width)], gb.at[m], sems.at[4])
        cp_g.start()
        scale_in = arr_v[:, pl.ds(width, 1)].astype(F32)

        zero = jnp.zeros((rows, BLK), F32)
        gh = zero
        for k in range(NF):
            gh = gh + jnp.dot(arr_v[:, cols(fb[k])], wu[k], preferred_element_type=F32)
        cp_pre.wait()
        cp_inv.wait()
        pre = pre_v[...]
        inv = inv_v[:, pl.ds(0, 1)]
        sigma = jax.nn.sigmoid(pre)
        grad_pre = gh * scale_in * sigma * (1.0 + pre * (1.0 - sigma))
        gp = grad_pre.astype(BF)
        gs_v[...] = (grad_pre * inv).astype(BF)
        hs_v[...] = (pre * sigma * scale_in).astype(BF)
        cp_gs = pltpu.make_async_copy(gs_v, qb.at[m], sems.at[5])
        cp_gs.start()
        cp_hs = pltpu.make_async_copy(hs_v, hb.at[m], sems.at[6])
        cp_hs.start()
        cp_x.wait()
        dots = zero
        for k in range(NF):
            c = cols(fa[k])
            gu = jnp.dot(gp, wd[k], preferred_element_type=F32)
            u_v[:, c] = gu
            dots = dots + gu * x_v[:, c].astype(F32)
        mean = jnp.sum(dots, axis=-1, keepdims=True) * inv * (1.0 / width)
        pull = inv * inv * mean

        def leave(i, top):
            c = cols(i)
            dx = scale_in * arr_v[:, c].astype(F32) + (
                inv * u_v[:, c] - pull * x_v[:, c].astype(F32)
            )
            u_v[:, c] = dx
            dx_v[:, c] = dx.astype(BF)
            return jnp.maximum(top, jnp.abs(dx))

        top = lax.fori_loop(0, NF, leave, zero, unroll=4)
        cp_dx = pltpu.make_async_copy(dx_v, xb.at[m], sems.at[7])
        cp_dx.start()
        scale_b = (jnp.max(top, axis=-1, keepdims=True) + TINY).astype(BF)
        inverse = 1.0 / scale_b.astype(F32)
        pk_v[:, pl.ds(width, CODE)] = jnp.broadcast_to(scale_b, (rows, CODE))

        def code(i, carry):
            c = cols(i)
            pk_v[:, c] = (u_v[:, c] * inverse).astype(BF)
            return carry

        lax.fori_loop(0, NF, code, 0, unroll=4)
        cp_pk = pltpu.make_async_copy(pk_v, pk, sems.at[0])
        cp_pk.start()
        cp_g.wait()
        cp_gs.wait()
        cp_hs.wait()
        cp_dx.wait()
        cp_pk.wait()


BIG = jax.ShapeDtypeStruct((3, 64, 8192), BF)
PRE = jax.ShapeDtypeStruct((3, 64, 256), F32)
INV = jax.ShapeDtypeStruct((3, 64, 128), F32)
GP = jax.ShapeDtypeStruct((3, 64, 256), BF)
WHOLE = jax.ShapeDtypeStruct((NF, 256, BLK), BF)
PK = jax.ShapeDtypeStruct((64, 8192 + CODE), BF)
WIDE = pltpu.VMEM((64, 8192), BF)
WIDE_F = pltpu.VMEM((64, 8192), F32)
CODED = pltpu.VMEM((64, 8192 + CODE), BF)
SMALL = [pltpu.VMEM((64, 256), F32), pltpu.VMEM((64, 128), F32)]
PARAMS = pltpu.CompilerParams(vmem_limit_bytes=VMEM_LIMIT)
COST = pl.CostEstimate(flops=4 * 64 * 8192 * 256, bytes_accessed=16 * 1024 * 1024, transcendentals=0)


def forward(tick, table, fa, fb, stores, weights, arrived, held):
    fresh = not arrived
    extra = tuple(arrived)
    n = 6 + len(extra) + len(weights)
    return pl.pallas_call(
        lambda *refs: forward_kernel(tick, fresh, *refs),
        out_shape=(BIG, BIG, PRE, INV, PK) + ((WHOLE, WHOLE) if fresh else ()),
        in_specs=[smem_spec()] * 3 + [hbm_spec()] * 3 + [any_spec()] * len(extra)
        + [any_spec() if fresh else weight_spec()] * len(weights) + [hbm_spec()] * len(held),
        out_specs=[hbm_spec()] * 4 + [any_spec()] + [weight_spec()] * (2 * fresh),
        scratch_shapes=[CODED, WIDE, WIDE, WIDE, WIDE_F, WIDE, CODED] + SMALL
        + [pltpu.SemaphoreType.DMA((8 + 2 * PIECES,))],
        input_output_aliases={n + i: i for i in range(len(held))},
        compiler_params=PARAMS,
        cost_estimate=COST,
        name="section_forward",
    )(table, fa, fb, *stores, *extra, *weights, *held)


def backward(tick, table, fa, fb, cot, weights, arrived, saved, held):
    fresh = not arrived
    extra = tuple(arrived)
    n = 4 + len(extra) + len(weights)
    return pl.pallas_call(
        lambda *refs: backward_kernel(tick, fresh, *refs),
        out_shape=(BIG, PRE, INV, BIG, BIG, GP, GP, PK),
        in_specs=[smem_spec()] * 3 + [hbm_spec()] + [any_spec()] * len(extra)
        + [weight_spec()] * len(weights) + [hbm_spec()] * (3 + len(held)),
        out_specs=[hbm_spec()] * 7 + [any_spec()],
        scratch_shapes=[CODED, WIDE, WIDE_F, WIDE, CODED] + SMALL
        + [pltpu.VMEM((64, 256), BF)] * 2 + [pltpu.SemaphoreType.DMA((8,))],
        input_output_aliases={n + i: i for i in range(3 + len(held))},
        compiler_params=PARAMS,
        cost_estimate=COST,
        name="section_backward",
    )(table, fa, fb, cot, *extra, *weights, *saved, *held)


def transpose_kernel(wd, wu, wd_t, wu_t):
    for k in range(NF):
        wd_t[k] = wd[k].T
        wu_t[k] = wu[k].T


def transposed(weights):
    return pl.pallas_call(
        transpose_kernel,
        out_shape=tuple(jax.ShapeDtypeStruct(w.shape, BF) for w in weights),
        in_specs=[weight_spec()] * len(weights),
        out_specs=[weight_spec()] * len(weights),
        compiler_params=PARAMS,
        cost_estimate=pl.CostEstimate(flops=0, bytes_accessed=16 * 1024 * 1024, transcendentals=0),
        name="transpose_weights",
    )(*weights)


def prepare(down, up, gain):
    def kernel(down_ref, up_ref, gain_ref, out_ref):
        column = jnp.broadcast_to(gain_ref[...].astype(F32), (BLK, BLK)).T
        out_ref[pl.ds(0, BLK), :] = (column * down_ref[0].astype(F32)).astype(BF)
        out_ref[pl.ds(BLK, BLK), :] = up_ref[0]

    return pl.pallas_call(
        kernel,
        out_shape=jax.ShapeDtypeStruct((2 * BLK, BLK), BF),
        in_specs=[weight_spec()] * 3,
        out_specs=weight_spec(),
        name="scale_weights",
    )(down, up, gain)


def finish(unit_terms, up_terms, down, gain):
    def kernel(*refs):
        n = len(unit_terms)
        down_ref, gain_ref, gain_out, down_out, up_out = refs[2 * n :]
        unit_t = sum(r[0].astype(F32) for r in refs[:n])
        up_out[0] = sum(r[0].astype(F32) for r in refs[n : 2 * n])
        gain_out[...] = jnp.sum(down_ref[0].astype(F32).T * unit_t, axis=0, keepdims=True)
        down_out[0] = (unit_t * gain_ref[...].astype(F32)).T

    return pl.pallas_call(
        kernel,
        out_shape=(
            jax.ShapeDtypeStruct((1, BLK), F32),
            jax.ShapeDtypeStruct((1, BLK, BLK), F32),
            jax.ShapeDtypeStruct((1, BLK, BLK), F32),
        ),
        in_specs=[weight_spec()] * (2 * len(unit_terms) + 2),
        out_specs=[weight_spec()] * 3,
        name="finish_gradients",
    )(*unit_terms, *up_terms, down, gain)


EARLY = ((2, 0), (2, 1), (1, 1), (3, 0))
LATE = ((1, 0), (3, 1), (0, 0), (0, 1))


def partial_kernel(parts, pos, x_hbm, g_hbm, hs_hbm, gs_hbm, *refs):
    outs, (x_v, g_v, hs_v, gs_v, ht_v, gt_v, out_a, out_b, sems, osems) = refs[:8], refs[8:]
    loads = []
    for i, (src, dst) in enumerate(((gs_hbm, gs_v), (hs_hbm, hs_v), (x_hbm, x_v), (g_hbm, g_v))):
        cp = pltpu.make_async_copy(src, dst, sems.at[i])
        cp.start()
        loads.append(cp)
    z, x, y = pos[0], pos[1], pos[2]
    loads[0].wait()
    loads[1].wait()
    ht_v[...] = hs_v[...].astype(F32).T.astype(BF)
    gt_v[...] = gs_v[...].astype(F32).T.astype(BF)
    loads[2].wait()
    loads[3].wait()
    stores = []
    for n, (step, half) in enumerate(parts):
        for e in range(4):
            other, kz = 2 * half + e // 2, e % 2
            zz = lax.rem(z + kz, NZ) * (NX * NY)
            c = cols(zz + lax.rem(x + other, NX) * NY + lax.rem(y + step, NY))
            out_a[n, e] = jnp.dot(gt_v[...], x_v[:, c], preferred_element_type=F32).astype(BF)
            c = cols(zz + lax.rem(x + step, NX) * NY + lax.rem(y + other, NY))
            out_b[n, e] = jnp.dot(ht_v[...], g_v[:, c], preferred_element_type=F32).astype(BF)
        for i, block in ((n, out_a.at[n]), (4 + n, out_b.at[n])):
            cp = pltpu.make_async_copy(block, outs[i], osems.at[i])
            cp.start()
            stores.append(cp)
    for cp in stores:
        cp.wait()


def partials(parts, pos, x_all, g_all, hs_all, gs_all):
    rows, width = x_all.shape
    group = jax.ShapeDtypeStruct((4, 256, BLK), BF)
    outs = pl.pallas_call(
        lambda *refs: partial_kernel(parts, *refs),
        out_shape=(group,) * 8,
        in_specs=[smem_spec()] + [hbm_spec()] * 4,
        out_specs=[any_spec()] * 8,
        scratch_shapes=[pltpu.VMEM((rows, width), BF)] * 2
        + [pltpu.VMEM((rows, 256), BF)] * 2
        + [pltpu.VMEM((256, rows), BF)] * 2
        + [pltpu.VMEM((4, 4, 256, BLK), BF)] * 2
        + [pltpu.SemaphoreType.DMA((4,)), pltpu.SemaphoreType.DMA((8,))],
        compiler_params=PARAMS,
        cost_estimate=pl.CostEstimate(
            flops=2 * rows * width * 256, bytes_accessed=10 * 1024 * 1024, transcendentals=0
        ),
        name="gradient_partials",
    )(pos, x_all, g_all, hs_all, gs_all)
    return dict(zip(parts, outs[:4])), dict(zip(parts, outs[4:]))


def gather_weights(own):
    far = shift(own, 1, 0, 0)

    def two_axes(pair, first, second):
        one, three, two = [shift(pair, *first(-d)) for d in (1, 3, 2)]
        lo, hi = jnp.concatenate([pair, one], axis=0), jnp.concatenate([three, two], axis=0)
        ahead_lo, behind_lo = shift(lo, *second(-1)), shift(lo, *second(1))
        behind_hi, ahead_hi = shift(hi, *second(1)), shift(hi, *second(-1))
        far_lo, far_hi = shift(ahead_lo, *second(-1)), shift(behind_hi, *second(1))
        places = [
            (d, e, kz)
            for e, ds in ((0, (0, 1)), (1, (0, 1)), (3, (0, 1)), (0, (3, 2)), (3, (3, 2)), (1, (3, 2)), (2, (0, 1)), (2, (3, 2)))
            for d in ds
            for kz in range(NZ)
        ]
        return places, (lo, ahead_lo, behind_lo, hi, behind_hi, ahead_hi, far_lo, far_hi)

    along_x = lambda d: (0, d, 0)
    along_y = lambda d: (0, 0, d)
    keys_a, wd = two_axes(jnp.stack([own[:BLK], far[:BLK]]), along_x, along_y)
    keys_b, wu = two_axes(jnp.stack([own[BLK:], far[BLK:]]), along_y, along_x)
    keys_a = [(kz, d, e) for d, e, kz in keys_a]
    keys_b = [(kz, e, d) for d, e, kz in keys_b]
    return keys_a, wd, keys_b, wu


LAG = (0, 1, 3, 4)
SOURCE = (0, 1, 2, 1)
ORDER = (
    [("forward", t) for t in range(4)]
    + [("transpose", 0)]
    + [(kind, t + 4 * (kind == "forward")) for t in range(3) for kind in ("forward", "backward")]
    + [("backward", t) for t in range(3, 7)]
)


def place(keys, z, x, y):
    keys = jnp.array(keys, jnp.int32)
    return (
        lax.rem(z + keys[:, 0], NZ) * (NX * NY)
        + lax.rem(x + keys[:, 1], NX) * NY
        + lax.rem(y + keys[:, 2], NY)
    ).astype(jnp.int32)


def add_up(*terms):
    return sum(t.astype(F32) for t in terms).astype(BF)


def scatter_two(part, first, second):
    far_lo, far_hi = shift(part[2, 0], *first(1)), shift(part[2, 1], *first(-1))
    up_hi, down_lo = shift(part[1, 1], *first(1)), shift(part[3, 0], *first(-1))
    up_lo = shift(add_up(part[1, 0], far_lo), *first(1))
    down_hi = shift(add_up(part[3, 1], far_hi), *first(-1))
    low = (part[0, 0], up_lo, down_lo)
    high = (part[0, 1], up_hi, down_hi)
    ahead = shift(add_up(*(t[2:4] for t in low)), *second(1))
    far = shift(add_up(*(t[0:2] for t in high)), *second(2))
    behind = shift(add_up(*(t[2:4] for t in high)), *second(-1))
    own = [t[0:2] for t in low]
    there = shift(add_up(*(t[1:2] for t in own), ahead[1:2], far[1:2], behind[1:2]), 1, 0, 0)
    here = add_up(*(t[0:1] for t in own), ahead[0:1], far[0:1], behind[0:1])
    return here, there


def per_device(entering, in_store, out_store, norm_gain, adapter_down, adapter_up, sample_ids, cotangent):
    n_sec = lax.axis_size("pipe")
    sec = lax.axis_index("pipe")
    f = lax.axis_index("fsdp")
    z, x, y = f // (NX * NY), lax.rem(f // NY, NX), lax.rem(f, NY)
    n_micro, rows, width = entering.shape

    keys_a, wd, keys_b, wu = gather_weights(prepare(adapter_down, adapter_up, norm_gain))
    fa, fb = place(keys_a, z, x, y), place(keys_b, z, x, y)
    weights = (*wd, *wu)

    lag = jnp.array(LAG, jnp.int32)
    ticks = n_micro + LAG[-1]
    step = jnp.arange(ticks, dtype=jnp.int32)
    m_f, m_b = step - lag[sec], step - lag[n_sec - 1 - sec]
    slot_f, slot_b = jnp.clip(m_f, 0, n_micro - 1), jnp.clip(m_b, 0, n_micro - 1)
    source_f, source_b = jnp.array(SOURCE, jnp.int32)[sec], jnp.array(SOURCE, jnp.int32)[n_sec - 1 - sec]
    table = jnp.stack(
        [
            (m_f >= 0) & (m_f < n_micro),
            slot_f,
            sample_ids[slot_f],
            jnp.broadcast_to(source_f, (ticks,)),
            (m_b >= 0) & (m_b < n_micro),
            slot_b,
            jnp.broadcast_to(source_b, (ticks,)),
            step,
        ],
        axis=1,
    ).astype(jnp.int32)

    def send(block, tick, hops, towards):
        edges = [hop[::towards] for hop in hops]
        live = [e for e in edges if 0 <= tick - LAG[e[0] if towards == 1 else n_sec - 1 - e[0]] < n_micro]
        return lax.ppermute(block, "pipe", live) if live else None

    def arrivals(near, far, tick):
        pair = (near.get(tick - 1), far.get(tick - 2))
        return tuple(p if p is not None else q for p, q in (pair, pair[::-1]) if p is not None or q is not None)

    stores = (entering, in_store[0], out_store[0])
    near_f, far_f, near_b, far_b = {}, {}, {}, {}
    held_f, held_b = (), ()
    weights_t = None
    for kind, tick in ORDER:
        if kind == "transpose":
            weights_t = transposed(weights)
        elif kind == "forward":
            *held_f, sent = forward(tick, table, fa, fb, stores, weights, arrivals(near_f, far_f, tick), held_f)
            if tick == 0:
                *held_f, sent, wd_all, wu_all = (*held_f, sent)
                weights = (wd_all, wu_all)
            near_f[tick] = send(sent, tick, ((0, 1), (2, 3)), 1)
            far_f[tick] = send(sent, tick, ((1, 2),), 1)
        else:
            ib, sb, pb, vb = held_f
            ib, pb, vb, *held_b, back = backward(
                tick, table, fa, fb, cotangent, weights_t, arrivals(near_b, far_b, tick), (ib, pb, vb), held_b
            )
            held_f = (ib, sb, pb, vb)
            near_b[tick] = send(back, tick, ((0, 1), (2, 3)), -1)
            far_b[tick] = send(back, tick, ((1, 2),), -1)
    ib, sb, pb, vb = held_f
    gb, xb, hb, qb = held_b

    all_rows = n_micro * rows
    pos = jnp.stack([z, x, y]).astype(jnp.int32)
    whole = [t.reshape(all_rows, -1) for t in (ib, gb, hb, qb)]
    early_a, early_b = partials(EARLY, pos, *whole)
    late_a, late_b = partials(LATE, pos, *whole)
    along_x = lambda d: (0, d, 0)
    along_y = lambda d: (0, 0, d)
    unit_terms = scatter_two({**early_a, **late_a}, along_y, along_x)
    up_terms = scatter_two({**early_b, **late_b}, along_x, along_y)
    grad_gain, grad_down, grad_up = finish(unit_terms, up_terms, adapter_down, norm_gain)
    return (
        sb[None],
        ib[None],
        xb[None],
        grad_gain,
        grad_down,
        grad_up,
    )


def solution(mesh):
    return jax.shard_map(
        per_device,
        mesh=mesh,
        in_specs=(
            P(None, "fsdp", None),
            P("pipe", None, "fsdp", None),
            P("pipe", None, "fsdp", None),
            P("pipe", "fsdp"),
            P("pipe", "fsdp", None),
            P("pipe", None, "fsdp"),
            P(),
            P(None, "fsdp", None),
        ),
        out_specs=(
            P("pipe", None, "fsdp", None),
            P("pipe", None, "fsdp", None),
            P("pipe", None, "fsdp", None),
            P("pipe", "fsdp"),
            P("pipe", "fsdp", None),
            P("pipe", None, "fsdp"),
        ),
        check_vma=False,
    )
```

```python
import jax
import jax.numpy as jnp
from jax import lax
from jax.experimental import pallas as pl
from jax.experimental.pallas import tpu as pltpu
from jax.sharding import PartitionSpec as P

EPS = 1e-05
TINY = 1e-06
NZ, NX, NY = 2, 4, 4
NF = NZ * NX * NY
BLK = 256
CODE = 128
F32 = jnp.float32
BF = jnp.bfloat16
VMEM_LIMIT = 12 * 1024 * 1024


def flat(z, x, y):
    return (z % NZ) * (NX * NY) + (x % NX) * NY + (y % NY)


def shift(block, dz, first, second):
    route = [
        (s * NF + flat(z, x, y), s * NF + flat(z + dz, x + (second if s % 2 else first), y + (first if s % 2 else second)))
        for s in range(4)
        for z in range(NZ)
        for x in range(NX)
        for y in range(NY)
    ]
    return lax.ppermute(block, ("pipe", "fsdp"), route)


def along(d):
    return (0, d, 0)


def across(d):
    return (0, 0, d)


def any_spec():
    return pl.BlockSpec(memory_space=pl.ANY)


def hbm_spec():
    return pl.BlockSpec(memory_space=pltpu.HBM)


def smem_spec():
    return pl.BlockSpec(memory_space=pltpu.SMEM)


def in_hbm(*arrays):
    return tuple(pltpu.with_memory_space_constraint(t, pltpu.HBM) for t in arrays)


def cols(index):
    return pl.ds(pl.multiple_of(index * BLK, BLK), BLK)


PIECES = 8
PER = NF // PIECES


def weight_spec():
    return pl.BlockSpec(memory_space=pltpu.VMEM)


def fetch(uncoded, arrivals, dst, sem, source):
    rows, width = uncoded.shape
    copies = [pltpu.make_async_copy(uncoded, dst.at[:, pl.ds(0, width)], sem)]
    copies += [pltpu.make_async_copy(arrival, dst, sem) for arrival in arrivals]
    for i, copy in enumerate(copies):
        pl.when(source == i)(copy.start)

    def wait():
        for i, copy in enumerate(copies):
            pl.when(source == i)(copy.wait)

        @pl.when(source == 0)
        def _():
            dst[:, width:] = jnp.ones((rows, CODE), BF)

    return wait


def forward_kernel(tick, fresh, *refs):
    at = 5 if fresh else 7
    s_ref, fa, ent, ins, outs = refs[:5]
    if fresh:
        n_in = at + PIECES
        pieces, (wd, wu) = refs[at:n_in], refs[n_in + 5 : n_in + 7]
        ib, sb, pb, vb, pk = refs[n_in : n_in + 5]
        scratch = refs[n_in + 7 :]
    else:
        wd, wu = refs[at : at + 2]
        n_in = at + 2 + 4
        ib, sb, pb, vb, pk = refs[n_in : n_in + 5]
        scratch = refs[n_in + 5 :]
    arr_v, out_v, x_v, v_v, ref_v, pre_v, inv_v, sems = scratch
    rows, width = x_v.shape
    live, m, j, source = s_ref[tick, 0], s_ref[tick, 1], s_ref[tick, 2], s_ref[tick, 3]
    loads = []
    if fresh:
        for n, whole in enumerate((wd, wu)):
            for i, piece in enumerate(pieces):
                half = piece.at[:, pl.ds(n * BLK, BLK), :]
                loads.append(pltpu.make_async_copy(half, whole.at[pl.ds(i * PER, PER)], sems.at[8 + n * PIECES + i]))

    @pl.when(live == 1)
    def _():
        cp_out = pltpu.make_async_copy(outs.at[j], out_v, sems.at[2])
        cp_out.start()
        await_arrival = fetch(ent.at[m], refs[5:at], arr_v, sems.at[1], source)
        for load in loads[:PIECES]:
            load.start()
        for load in loads[PIECES:]:
            load.start()

        await_arrival()

        scale_in = arr_v[:, pl.ds(width, 1)].astype(F32)
        zero = jnp.zeros((rows, BLK), F32)
        square = pre = zero
        for k in range(NF):
            if fresh and k % PER == 0:
                loads[k // PER].wait()
            c = cols(fa[k])
            x = (ins[j, :, c].astype(F32) + scale_in * arr_v[:, c].astype(F32)).astype(BF)
            x_v[:, c] = x
            xf = x.astype(F32)
            square = square + xf * xf
            pre = pre + jnp.dot(x, wd[k], preferred_element_type=F32)
        cp_x = pltpu.make_async_copy(x_v, ib.at[m], sems.at[3])
        cp_x.start()
        inv = lax.rsqrt(jnp.sum(square, axis=-1, keepdims=True) * (1.0 / width) + EPS)
        inv_v[...] = jnp.broadcast_to(inv, inv_v.shape)
        pre = pre * inv
        pre_v[...] = pre
        hidden = (pre * jax.nn.sigmoid(pre)).astype(BF)
        cp_pre = pltpu.make_async_copy(pre_v, pb.at[m], sems.at[4])
        cp_pre.start()
        cp_inv = pltpu.make_async_copy(inv_v, vb.at[m], sems.at[5])
        cp_inv.start()

        cp_out.wait()
        top = zero
        for k in range(NF):
            if fresh and k % PER == 0:
                loads[PIECES + k // PER].wait()
            c = cols(fa[k])
            v = (
                x_v[:, c].astype(F32)
                + jnp.dot(hidden, wu[k], preferred_element_type=F32)
                - out_v[:, c].astype(F32)
            )
            v_v[:, c] = v
            top = jnp.maximum(top, jnp.abs(v))
        scale_b = (jnp.max(top, axis=-1, keepdims=True) + TINY).astype(BF)
        scale = scale_b.astype(F32)
        inverse = 1.0 / scale
        pk[:, pl.ds(width, CODE)] = jnp.broadcast_to(scale_b, (rows, CODE))

        def code(i, carry):
            c = cols(i)
            packed = (v_v[:, c] * inverse).astype(BF)
            pk[:, c] = packed
            ref_v[:, c] = (out_v[:, c].astype(F32) + scale * packed.astype(F32)).astype(BF)
            return carry

        cp_refs = []
        for q in range(4):
            lax.fori_loop(q * NF // 4, (q + 1) * NF // 4, code, 0, unroll=4)
            part = pl.ds(q * width // 4, width // 4)
            cp = pltpu.make_async_copy(ref_v.at[:, part], sb.at[m, :, part], sems.at[(0, 2, 6, 7)[q]])
            cp.start()
            cp_refs.append(cp)
        cp_x.wait()
        cp_pre.wait()
        cp_inv.wait()
        for cp in cp_refs:
            cp.wait()

    if fresh:

        @pl.when(live == 0)
        def _():
            for load in loads:
                load.start()
            for load in loads:
                load.wait()


def backward_kernel(tick, fresh, *refs):
    at = 3 if fresh else 5
    s_ref, fa, cot = refs[:3]
    wd, wu = refs[at : at + 2]
    n_in = at + 2 + 3 + (0 if fresh else 4)
    ib, pb, vb, gb, xb, hb, qb, pk = refs[n_in : n_in + 8]
    arr_v, x_v, u_v, dx_v, pre_v, inv_v, hs_v, gs_v, sems = refs[n_in + 8 :]
    rows, width = x_v.shape
    live, m, source = s_ref[tick, 4], s_ref[tick, 5], s_ref[tick, 6]

    @pl.when(live == 1)
    def _():
        await_arrival = fetch(cot.at[m], refs[3:at], arr_v, sems.at[1], source)
        cp_x = pltpu.make_async_copy(ib.at[m], x_v, sems.at[0])
        cp_pre = pltpu.make_async_copy(pb.at[m], pre_v, sems.at[2])
        cp_inv = pltpu.make_async_copy(vb.at[m], inv_v, sems.at[3])
        cp_pre.start()
        cp_inv.start()
        cp_x.start()
        await_arrival()
        cp_g = pltpu.make_async_copy(arr_v.at[:, pl.ds(0, width)], gb.at[m], sems.at[4])
        cp_g.start()
        scale_in = arr_v[:, pl.ds(width, 1)].astype(F32)

        zero = jnp.zeros((rows, BLK), F32)
        gh = zero
        for k in range(NF):
            gh = gh + jnp.dot(arr_v[:, cols(fa[k])], wu[k], preferred_element_type=F32)
        cp_pre.wait()
        cp_inv.wait()
        pre = pre_v[...]
        inv = inv_v[:, pl.ds(0, 1)]
        sigma = jax.nn.sigmoid(pre)
        grad_pre = gh * scale_in * sigma * (1.0 + pre * (1.0 - sigma))
        gp = grad_pre.astype(BF)
        gs_v[...] = (grad_pre * inv).astype(BF)
        hs_v[...] = (pre * sigma * scale_in).astype(BF)
        cp_gs = pltpu.make_async_copy(gs_v, qb.at[m], sems.at[5])
        cp_gs.start()
        cp_hs = pltpu.make_async_copy(hs_v, hb.at[m], sems.at[6])
        cp_hs.start()
        cp_x.wait()
        dots = zero
        for k in range(NF):
            c = cols(fa[k])
            gu = jnp.dot(gp, wd[k], preferred_element_type=F32)
            u_v[:, c] = gu
            dots = dots + gu * x_v[:, c].astype(F32)
        mean = jnp.sum(dots, axis=-1, keepdims=True) * inv * (1.0 / width)
        pull = inv * inv * mean

        def leave(i, top):
            c = cols(i)
            dx = scale_in * arr_v[:, c].astype(F32) + (
                inv * u_v[:, c] - pull * x_v[:, c].astype(F32)
            )
            u_v[:, c] = dx
            dx_v[:, c] = dx.astype(BF)
            return jnp.maximum(top, jnp.abs(dx))

        top = lax.fori_loop(0, NF, leave, zero, unroll=4)
        cp_dx = pltpu.make_async_copy(dx_v, xb.at[m], sems.at[7])
        cp_dx.start()
        scale_b = (jnp.max(top, axis=-1, keepdims=True) + TINY).astype(BF)
        inverse = 1.0 / scale_b.astype(F32)
        pk[:, pl.ds(width, CODE)] = jnp.broadcast_to(scale_b, (rows, CODE))

        def code(i, carry):
            c = cols(i)
            pk[:, c] = (u_v[:, c] * inverse).astype(BF)
            return carry

        lax.fori_loop(0, NF, code, 0, unroll=4)
        cp_g.wait()
        cp_gs.wait()
        cp_hs.wait()
        cp_dx.wait()


BIG = jax.ShapeDtypeStruct((3, 64, 8192), BF)
PRE = jax.ShapeDtypeStruct((3, 64, 256), F32)
INV = jax.ShapeDtypeStruct((3, 64, 128), F32)
GP = jax.ShapeDtypeStruct((3, 64, 256), BF)
HELD = pltpu.VMEM((NF, 256, BLK), BF)
PK = jax.ShapeDtypeStruct((64, 8192 + CODE), BF)
WIDE = pltpu.VMEM((64, 8192), BF)
WIDE_F = pltpu.VMEM((64, 8192), F32)
CODED = pltpu.VMEM((64, 8192 + CODE), BF)
SMALL = [pltpu.VMEM((64, 256), F32), pltpu.VMEM((64, 128), F32)]
PARAMS = pltpu.CompilerParams(vmem_limit_bytes=VMEM_LIMIT)
COST = pl.CostEstimate(flops=4 * 64 * 8192 * 256, bytes_accessed=16 * 1024 * 1024, transcendentals=0)


def forward(tick, table, fa, stores, weights, arrived, held):
    fresh = not arrived
    extra = tuple(arrived)
    n = 5 + len(extra) + len(weights)
    return pl.pallas_call(
        lambda *refs: forward_kernel(tick, fresh, *refs),
        out_shape=(BIG, BIG, PRE, INV, PK) + ((HELD, HELD) if fresh else ()),
        in_specs=[smem_spec()] * 2 + [hbm_spec()] + [weight_spec(), hbm_spec()] + [any_spec()] * len(extra)
        + [any_spec() if fresh else weight_spec()] * len(weights) + [hbm_spec()] * len(held),
        out_specs=[hbm_spec()] * 4 + [weight_spec()] + [weight_spec()] * (2 * fresh),
        scratch_shapes=[CODED, WIDE, WIDE, WIDE_F, WIDE] + SMALL
        + [pltpu.SemaphoreType.DMA((8 + 2 * PIECES,))],
        input_output_aliases={n + i: i for i in range(len(held))},
        compiler_params=PARAMS,
        cost_estimate=COST,
        name="section_forward",
    )(table, fa, *in_hbm(stores[0]), stores[1], *in_hbm(stores[2]), *extra, *weights, *held)


def backward(tick, table, fa, cot, weights, arrived, saved, held):
    fresh = not arrived
    extra = tuple(arrived)
    n = 3 + len(extra) + len(weights)
    return pl.pallas_call(
        lambda *refs: backward_kernel(tick, fresh, *refs),
        out_shape=(BIG, PRE, INV, BIG, BIG, GP, GP, PK),
        in_specs=[smem_spec()] * 2 + [hbm_spec()] + [any_spec()] * len(extra)
        + [weight_spec()] * len(weights) + [hbm_spec()] * (3 + len(held)),
        out_specs=[hbm_spec()] * 7 + [weight_spec()],
        scratch_shapes=[CODED, WIDE, WIDE_F, WIDE] + SMALL
        + [pltpu.VMEM((64, 256), BF)] * 2 + [pltpu.SemaphoreType.DMA((8,))],
        input_output_aliases={n + i: i for i in range(3 + len(held))},
        compiler_params=PARAMS,
        cost_estimate=COST,
        name="section_backward",
    )(table, fa, *in_hbm(cot), *extra, *weights, *saved, *held)


def transpose_kernel(wd, wu, wd_t, wu_t):
    for k in range(NF):
        wd_t[k] = wd[k].T
        wu_t[k] = wu[k].T


def transposed(weights):
    return pl.pallas_call(
        transpose_kernel,
        out_shape=(HELD,) * len(weights),
        in_specs=[weight_spec()] * len(weights),
        out_specs=[weight_spec()] * len(weights),
        compiler_params=PARAMS,
        cost_estimate=pl.CostEstimate(flops=0, bytes_accessed=16 * 1024 * 1024, transcendentals=0),
        name="transpose_weights",
    )(*weights)


def staged(store, after):
    def kernel(store_ref, _, store_v, sem):
        copy = pltpu.make_async_copy(store_ref, store_v, sem)
        copy.start()
        copy.wait()

    return pl.pallas_call(
        kernel,
        out_shape=pltpu.VMEM(BIG.shape, BF),
        in_specs=[hbm_spec(), any_spec()],
        out_specs=weight_spec(),
        scratch_shapes=[pltpu.SemaphoreType.DMA],
        compiler_params=PARAMS,
        name="stage_store",
    )(*in_hbm(store), after)


def prepare(down, up, gain):
    def kernel(down_ref, up_ref, gain_ref, out_ref):
        column = jnp.broadcast_to(gain_ref[...].astype(F32), (BLK, BLK)).T
        out_ref[pl.ds(0, BLK), :] = (column * down_ref[0].astype(F32)).astype(BF)
        out_ref[pl.ds(BLK, BLK), :] = up_ref[0]

    return pl.pallas_call(
        kernel,
        out_shape=jax.ShapeDtypeStruct((2 * BLK, BLK), BF),
        in_specs=[weight_spec()] * 3,
        out_specs=weight_spec(),
        name="scale_weights",
    )(down, up, gain)


def finish(terms, down, gain):
    def kernel(here, there, down_ref, gain_ref, gain_out, down_out, up_out):
        def total(rows):
            return here[0, rows, :].astype(F32) + there[0, rows, :].astype(F32)

        unit_t = total(pl.ds(0, BLK))
        up_out[0] = total(pl.ds(BLK, BLK))
        gain_out[...] = jnp.sum(down_ref[0].astype(F32).T * unit_t, axis=0, keepdims=True)
        down_out[0] = (unit_t * gain_ref[...].astype(F32)).T

    return pl.pallas_call(
        kernel,
        out_shape=(
            jax.ShapeDtypeStruct((1, BLK), F32),
            jax.ShapeDtypeStruct((1, BLK, BLK), F32),
            jax.ShapeDtypeStruct((1, BLK, BLK), F32),
        ),
        in_specs=[weight_spec()] * 4,
        out_specs=[weight_spec()] * 3,
        name="finish_gradients",
    )(*terms, down, gain)


EARLY = ((2, 0), (2, 1), (1, 1), (3, 0))
LATE = ((1, 0), (3, 1), (0, 0), (0, 1))


def partial_kernel(parts, pos, x_hbm, g_hbm, hs_hbm, gs_hbm, *refs):
    outs, (x_v, g_v, hs_v, gs_v, ht_v, gt_v, out_v, sems, osems) = refs[:4], refs[4:]
    loads = []
    for i, (src, dst) in enumerate(((gs_hbm, gs_v), (hs_hbm, hs_v), (x_hbm, x_v), (g_hbm, g_v))):
        cp = pltpu.make_async_copy(src, dst, sems.at[i])
        cp.start()
        loads.append(cp)
    z, x, y, odd = pos[0], pos[1], pos[2], pos[3]
    loads[0].wait()
    loads[1].wait()
    ht_v[...] = hs_v[...].astype(F32).T.astype(BF)
    gt_v[...] = gs_v[...].astype(F32).T.astype(BF)
    loads[2].wait()
    loads[3].wait()
    stores = []
    for n, (step, half) in enumerate(parts):
        for e in range(4):
            other, kz = 2 * half + e // 2, e % 2
            dx, dy = step + odd * (other - step), other + odd * (step - other)
            c = cols(lax.rem(z + kz, NZ) * (NX * NY) + lax.rem(x + dx, NX) * NY + lax.rem(y + dy, NY))
            out_v[n, e, pl.ds(0, BLK), :] = jnp.dot(gt_v[...], x_v[:, c], preferred_element_type=F32).astype(BF)
            out_v[n, e, pl.ds(BLK, BLK), :] = jnp.dot(ht_v[...], g_v[:, c], preferred_element_type=F32).astype(BF)
        cp = pltpu.make_async_copy(out_v.at[n], outs[n], osems.at[n])
        cp.start()
        stores.append(cp)
    for cp in stores:
        cp.wait()


def partials(parts, pos, x_all, g_all, hs_all, gs_all):
    rows, width = x_all.shape
    group = jax.ShapeDtypeStruct((4, 2 * BLK, BLK), BF)
    outs = pl.pallas_call(
        lambda *refs: partial_kernel(parts, *refs),
        out_shape=(group,) * 4,
        in_specs=[smem_spec()] + [hbm_spec()] * 4,
        out_specs=[any_spec()] * 4,
        scratch_shapes=[pltpu.VMEM((rows, width), BF)] * 2
        + [pltpu.VMEM((rows, 256), BF)] * 2
        + [pltpu.VMEM((256, rows), BF)] * 2
        + [pltpu.VMEM((4, 4, 2 * BLK, BLK), BF)]
        + [pltpu.SemaphoreType.DMA((4,)), pltpu.SemaphoreType.DMA((4,))],
        compiler_params=PARAMS,
        cost_estimate=pl.CostEstimate(
            flops=2 * rows * width * 256, bytes_accessed=10 * 1024 * 1024, transcendentals=0
        ),
        name="gradient_partials",
    )(pos, x_all, g_all, hs_all, gs_all)
    return dict(zip(parts, outs))


def gather_weights(own):
    pair = jnp.stack([own, shift(own, 1, 0, 0)])
    two, one, three = [shift(pair, *along(-d)) for d in (2, 1, 3)]
    lo, hi = jnp.concatenate([pair, one], axis=0), jnp.concatenate([three, two], axis=0)
    ahead_lo, behind_lo = shift(lo, *across(-1)), shift(lo, *across(1))
    behind_hi, ahead_hi = shift(hi, *across(1)), shift(hi, *across(-1))
    far_lo, far_hi = shift(ahead_lo, *across(-1)), shift(behind_hi, *across(1))
    low, high = (0, 1), (3, 2)
    places = [
        (kz, d, e)
        for e, ds in ((0, low), (1, low), (3, low), (0, high), (3, high), (1, high), (2, low), (2, high))
        for d in ds
        for kz in range(NZ)
    ]
    return places, (lo, ahead_lo, behind_lo, hi, behind_hi, ahead_hi, far_lo, far_hi), pair


LAG = (0, 1, 3, 4)
SOURCE = (0, 1, 2, 1)
ORDER = (
    [("forward", t) for t in range(4)]
    + [("transpose", 0)]
    + [(kind, t + 4 * (kind == "forward")) for t in range(3) for kind in ("forward", "backward")]
    + [("backward", t) for t in range(3, 7)]
)


def place(keys, z, x, y, odd):
    keys = jnp.array(keys, jnp.int32)
    dx, dy = jnp.where(odd, keys[:, 2], keys[:, 1]), jnp.where(odd, keys[:, 1], keys[:, 2])
    return (lax.rem(z + keys[:, 0], NZ) * (NX * NY) + lax.rem(x + dx, NX) * NY + lax.rem(y + dy, NY)).astype(jnp.int32)


def add_up(*terms):
    return sum(t.astype(F32) for t in terms).astype(BF)


def scatter(part):
    far_lo, far_hi = shift(part[2, 0], *along(1)), shift(part[2, 1], *along(-1))
    up_hi, down_lo = shift(part[1, 1], *along(1)), shift(part[3, 0], *along(-1))
    up_lo = shift(add_up(part[1, 0], far_lo), *along(1))
    down_hi = shift(add_up(part[3, 1], far_hi), *along(-1))
    low = (part[0, 0], up_lo, down_lo)
    high = (part[0, 1], up_hi, down_hi)
    far = shift(add_up(*(t[0:2] for t in high)), *across(2))
    behind = shift(add_up(*(t[2:4] for t in high)), *across(-1))
    ahead = shift(add_up(*(t[2:4] for t in low)), *across(1))
    own = [t[0:2] for t in low]
    there = shift(add_up(*(t[1:2] for t in own), ahead[1:2], far[1:2], behind[1:2]), 1, 0, 0)
    here = add_up(*(t[0:1] for t in own), ahead[0:1], far[0:1], behind[0:1])
    return here, there


def per_device(entering, in_store, out_store, norm_gain, adapter_down, adapter_up, sample_ids, cotangent):
    n_sec = lax.axis_size("pipe")
    sec = lax.axis_index("pipe")
    f = lax.axis_index("fsdp")
    z, x, y = f // (NX * NY), lax.rem(f // NY, NX), lax.rem(f, NY)
    n_micro, rows, width = entering.shape

    odd = lax.rem(sec, 2)
    keys, weights, pair = gather_weights(prepare(adapter_down, adapter_up, norm_gain))
    fa = place(keys, z, x, y, odd == 1)

    lag = jnp.array(LAG, jnp.int32)
    ticks = n_micro + LAG[-1]
    step = jnp.arange(ticks, dtype=jnp.int32)
    m_f, m_b = step - lag[sec], step - lag[n_sec - 1 - sec]
    slot_f, slot_b = jnp.clip(m_f, 0, n_micro - 1), jnp.clip(m_b, 0, n_micro - 1)
    source_f, source_b = jnp.array(SOURCE, jnp.int32)[sec], jnp.array(SOURCE, jnp.int32)[n_sec - 1 - sec]
    table = jnp.stack(
        [
            (m_f >= 0) & (m_f < n_micro),
            slot_f,
            sample_ids[slot_f],
            jnp.broadcast_to(source_f, (ticks,)),
            (m_b >= 0) & (m_b < n_micro),
            slot_b,
            jnp.broadcast_to(source_b, (ticks,)),
            step,
        ],
        axis=1,
    ).astype(jnp.int32)

    def send(block, tick, hops, towards):
        edges = [hop[::towards] for hop in hops]
        live = [e for e in edges if 0 <= tick - LAG[e[0] if towards == 1 else n_sec - 1 - e[0]] < n_micro]
        return lax.ppermute(block, "pipe", live) if live else None

    def arrivals(near, far, tick):
        pair = (near.get(tick - 1), far.get(tick - 2))
        return tuple(p if p is not None else q for p, q in (pair, pair[::-1]) if p is not None or q is not None)

    stores = (entering, staged(in_store[0], pair), out_store[0])
    near_f, far_f, near_b, far_b = {}, {}, {}, {}
    held_f, held_b = (), ()
    weights_t = None
    for kind, tick in ORDER:
        if kind == "transpose":
            weights_t = transposed(weights)
        elif kind == "forward":
            *held_f, sent = forward(tick, table, fa, stores, weights, arrivals(near_f, far_f, tick), held_f)
            if tick == 0:
                *held_f, sent, wd_all, wu_all = (*held_f, sent)
                weights = (wd_all, wu_all)
            near_f[tick] = send(sent, tick, ((0, 1), (2, 3)), 1)
            far_f[tick] = send(sent, tick, ((1, 2),), 1)
        else:
            ib, sb, pb, vb = held_f
            ib, pb, vb, *held_b, back = backward(
                tick, table, fa, cotangent, weights_t, arrivals(near_b, far_b, tick), (ib, pb, vb), held_b
            )
            held_f = (ib, sb, pb, vb)
            near_b[tick] = send(back, tick, ((0, 1), (2, 3)), -1)
            far_b[tick] = send(back, tick, ((1, 2),), -1)
    ib, sb, pb, vb = held_f
    gb, xb, hb, qb = held_b

    all_rows = n_micro * rows
    pos = jnp.stack([z, x, y, odd]).astype(jnp.int32)
    whole = [t.reshape(all_rows, -1) for t in (ib, gb, hb, qb)]
    parts = {**partials(EARLY, pos, *whole), **partials(LATE, pos, *whole)}
    grad_gain, grad_down, grad_up = finish(scatter(parts), adapter_down, norm_gain)
    return (
        sb[None],
        ib[None],
        xb[None],
        grad_gain,
        grad_down,
        grad_up,
    )


def solution(mesh):
    return jax.shard_map(
        per_device,
        mesh=mesh,
        in_specs=(
            P(None, "fsdp", None),
            P("pipe", None, "fsdp", None),
            P("pipe", None, "fsdp", None),
            P("pipe", "fsdp"),
            P("pipe", "fsdp", None),
            P("pipe", None, "fsdp"),
            P(),
            P(None, "fsdp", None),
        ),
        out_specs=(
            P("pipe", None, "fsdp", None),
            P("pipe", None, "fsdp", None),
            P("pipe", None, "fsdp", None),
            P("pipe", "fsdp"),
            P("pipe", "fsdp", None),
            P("pipe", None, "fsdp"),
        ),
        check_vma=False,
    )
```

```python
import jax
import jax.numpy as jnp
from jax import lax
from jax.experimental import pallas as pl
from jax.experimental.pallas import tpu as pltpu
from jax.sharding import PartitionSpec as P

EPS = 1e-05
TINY = 1e-06
NZ, NX, NY = 2, 4, 4
NF = NZ * NX * NY
BLK = 256
CODE = 128
F32 = jnp.float32
BF = jnp.bfloat16
VMEM_LIMIT = 12 * 1024 * 1024


def flat(z, x, y):
    return (z % NZ) * (NX * NY) + (x % NX) * NY + (y % NY)


def shift(block, dz, first, second):
    route = [
        (s * NF + flat(z, x, y), s * NF + flat(z + dz, x + (second if s % 2 else first), y + (first if s % 2 else second)))
        for s in range(4)
        for z in range(NZ)
        for x in range(NX)
        for y in range(NY)
    ]
    return lax.ppermute(block, ("pipe", "fsdp"), route)


def along(d):
    return (0, d, 0)


def across(d):
    return (0, 0, d)


def any_spec():
    return pl.BlockSpec(memory_space=pl.ANY)


def hbm_spec():
    return pl.BlockSpec(memory_space=pltpu.HBM)


def smem_spec():
    return pl.BlockSpec(memory_space=pltpu.SMEM)


def in_hbm(*arrays):
    return tuple(pltpu.with_memory_space_constraint(t, pltpu.HBM) for t in arrays)


def cols(index):
    return pl.ds(pl.multiple_of(index * BLK, BLK), BLK)


PIECES = 8
PER = NF // PIECES
UNROLL = 8


def blocks(body, init, before=None):
    carry = init
    if before is None:
        return lax.fori_loop(0, NF, body, carry, unroll=UNROLL)
    for i, copy in enumerate(before):
        copy.wait()
        carry = lax.fori_loop(i * PER, (i + 1) * PER, body, carry, unroll=True)
    return carry


def weight_spec():
    return pl.BlockSpec(memory_space=pltpu.VMEM)


def fetch(uncoded, arrivals, dst, sem, source):
    rows, width = uncoded.shape
    copies = [pltpu.make_async_copy(uncoded, dst.at[:, pl.ds(0, width)], sem)]
    copies += [pltpu.make_async_copy(arrival, dst, sem) for arrival in arrivals]
    for i, copy in enumerate(copies):
        pl.when(source == i)(copy.start)

    def wait():
        for i, copy in enumerate(copies):
            pl.when(source == i)(copy.wait)

        @pl.when(source == 0)
        def _():
            dst[:, width:] = jnp.ones((rows, CODE), BF)

    return wait


def forward_kernel(tick, fresh, *refs):
    at = 5 if fresh else 7
    s_ref, fa, ent, ins, outs = refs[:5]
    if fresh:
        n_in = at + PIECES
        pieces, (wd, wu) = refs[at:n_in], refs[n_in + 5 : n_in + 7]
        ib, sb, pb, vb, pk = refs[n_in : n_in + 5]
        scratch = refs[n_in + 7 :]
    else:
        wd, wu = refs[at : at + 2]
        n_in = at + 2 + 4
        ib, sb, pb, vb, pk = refs[n_in : n_in + 5]
        scratch = refs[n_in + 5 :]
    arr_v, out_v, x_v, v_v, ref_v, pre_v, inv_v, sems = scratch
    rows, width = x_v.shape
    live, m, j, source = s_ref[tick, 0], s_ref[tick, 1], s_ref[tick, 2], s_ref[tick, 3]
    loads = []
    if fresh:
        for n, whole in enumerate((wd, wu)):
            for i, piece in enumerate(pieces):
                half = piece.at[:, pl.ds(n * BLK, BLK), :]
                loads.append(pltpu.make_async_copy(half, whole.at[pl.ds(i * PER, PER)], sems.at[8 + n * PIECES + i]))

    @pl.when(live == 1)
    def _():
        cp_out = pltpu.make_async_copy(outs.at[j], out_v, sems.at[2])
        cp_out.start()
        await_arrival = fetch(ent.at[m], refs[5:at], arr_v, sems.at[1], source)
        for load in loads[:PIECES]:
            load.start()
        for load in loads[PIECES:]:
            load.start()

        await_arrival()

        scale_in = arr_v[:, pl.ds(width, 1)].astype(F32)
        zero = jnp.zeros((rows, BLK), F32)

        def enter(k, carry):
            square, pre = carry
            c = cols(fa[k])
            x = (ins[j, :, c].astype(F32) + scale_in * arr_v[:, c].astype(F32)).astype(BF)
            x_v[:, c] = x
            xf = x.astype(F32)
            return square + xf * xf, pre + jnp.dot(x, wd[k], preferred_element_type=F32)

        square, pre = blocks(enter, (zero, zero), loads[:PIECES] or None)
        cp_x = pltpu.make_async_copy(x_v, ib.at[m], sems.at[3])
        cp_x.start()
        inv = lax.rsqrt(jnp.sum(square, axis=-1, keepdims=True) * (1.0 / width) + EPS)
        inv_v[...] = jnp.broadcast_to(inv, inv_v.shape)
        pre = pre * inv
        pre_v[...] = pre
        hidden = (pre * jax.nn.sigmoid(pre)).astype(BF)
        cp_pre = pltpu.make_async_copy(pre_v, pb.at[m], sems.at[4])
        cp_pre.start()
        cp_inv = pltpu.make_async_copy(inv_v, vb.at[m], sems.at[5])
        cp_inv.start()

        cp_out.wait()

        def leave(k, top):
            c = cols(fa[k])
            v = (
                x_v[:, c].astype(F32)
                + jnp.dot(hidden, wu[k], preferred_element_type=F32)
                - out_v[:, c].astype(F32)
            )
            v_v[:, c] = v
            return jnp.maximum(top, jnp.abs(v))

        top = blocks(leave, zero, loads[PIECES:] or None)
        scale_b = (jnp.max(top, axis=-1, keepdims=True) + TINY).astype(BF)
        scale = scale_b.astype(F32)
        inverse = 1.0 / scale
        pk[:, pl.ds(width, CODE)] = jnp.broadcast_to(scale_b, (rows, CODE))

        def code(i, carry):
            c = cols(i)
            packed = (v_v[:, c] * inverse).astype(BF)
            pk[:, c] = packed
            ref_v[:, c] = (out_v[:, c].astype(F32) + scale * packed.astype(F32)).astype(BF)
            return carry

        cp_refs = []
        for q in range(4):
            lax.fori_loop(q * NF // 4, (q + 1) * NF // 4, code, 0, unroll=4)
            part = pl.ds(q * width // 4, width // 4)
            cp = pltpu.make_async_copy(ref_v.at[:, part], sb.at[m, :, part], sems.at[(0, 2, 6, 7)[q]])
            cp.start()
            cp_refs.append(cp)
        cp_x.wait()
        cp_pre.wait()
        cp_inv.wait()
        for cp in cp_refs:
            cp.wait()

    if fresh:

        @pl.when(live == 0)
        def _():
            for load in loads:
                load.start()
            for load in loads:
                load.wait()


def backward_kernel(tick, fresh, *refs):
    at = 3 if fresh else 5
    s_ref, fa, cot = refs[:3]
    wd, wu = refs[at : at + 2]
    n_in = at + 2 + 3 + (0 if fresh else 4)
    ib, pb, vb, gb, xb, hb, qb, pk = refs[n_in : n_in + 8]
    arr_v, x_v, u_v, dx_v, pre_v, inv_v, hs_v, gs_v, sems = refs[n_in + 8 :]
    rows, width = x_v.shape
    live, m, source = s_ref[tick, 4], s_ref[tick, 5], s_ref[tick, 6]

    @pl.when(live == 1)
    def _():
        await_arrival = fetch(cot.at[m], refs[3:at], arr_v, sems.at[1], source)
        cp_x = pltpu.make_async_copy(ib.at[m], x_v, sems.at[0])
        cp_pre = pltpu.make_async_copy(pb.at[m], pre_v, sems.at[2])
        cp_inv = pltpu.make_async_copy(vb.at[m], inv_v, sems.at[3])
        cp_pre.start()
        cp_inv.start()
        cp_x.start()
        await_arrival()
        cp_g = pltpu.make_async_copy(arr_v.at[:, pl.ds(0, width)], gb.at[m], sems.at[4])
        cp_g.start()
        scale_in = arr_v[:, pl.ds(width, 1)].astype(F32)

        zero = jnp.zeros((rows, BLK), F32)

        def enter(k, gh):
            return gh + jnp.dot(arr_v[:, cols(fa[k])], wu[k], preferred_element_type=F32)

        gh = blocks(enter, zero)
        cp_pre.wait()
        cp_inv.wait()
        pre = pre_v[...]
        inv = inv_v[:, pl.ds(0, 1)]
        sigma = jax.nn.sigmoid(pre)
        grad_pre = gh * scale_in * sigma * (1.0 + pre * (1.0 - sigma))
        gp = grad_pre.astype(BF)
        gs_v[...] = (grad_pre * inv).astype(BF)
        hs_v[...] = (pre * sigma * scale_in).astype(BF)
        cp_gs = pltpu.make_async_copy(gs_v, qb.at[m], sems.at[5])
        cp_gs.start()
        cp_hs = pltpu.make_async_copy(hs_v, hb.at[m], sems.at[6])
        cp_hs.start()
        cp_x.wait()

        def pull_back(k, dots):
            c = cols(fa[k])
            gu = jnp.dot(gp, wd[k], preferred_element_type=F32)
            u_v[:, c] = gu
            return dots + gu * x_v[:, c].astype(F32)

        dots = blocks(pull_back, zero)
        mean = jnp.sum(dots, axis=-1, keepdims=True) * inv * (1.0 / width)
        pull = inv * inv * mean

        def leave(i, top):
            c = cols(i)
            dx = scale_in * arr_v[:, c].astype(F32) + (
                inv * u_v[:, c] - pull * x_v[:, c].astype(F32)
            )
            u_v[:, c] = dx
            dx_v[:, c] = dx.astype(BF)
            return jnp.maximum(top, jnp.abs(dx))

        top = lax.fori_loop(0, NF, leave, zero, unroll=4)
        cp_dx = pltpu.make_async_copy(dx_v, xb.at[m], sems.at[7])
        cp_dx.start()
        scale_b = (jnp.max(top, axis=-1, keepdims=True) + TINY).astype(BF)
        inverse = 1.0 / scale_b.astype(F32)
        pk[:, pl.ds(width, CODE)] = jnp.broadcast_to(scale_b, (rows, CODE))

        def code(i, carry):
            c = cols(i)
            pk[:, c] = (u_v[:, c] * inverse).astype(BF)
            return carry

        lax.fori_loop(0, NF, code, 0, unroll=4)
        cp_g.wait()
        cp_gs.wait()
        cp_hs.wait()
        cp_dx.wait()


BIG = jax.ShapeDtypeStruct((3, 64, 8192), BF)
PRE = jax.ShapeDtypeStruct((3, 64, 256), F32)
INV = jax.ShapeDtypeStruct((3, 64, 128), F32)
GP = jax.ShapeDtypeStruct((3, 64, 256), BF)
HELD = pltpu.VMEM((NF, 256, BLK), BF)
PK = jax.ShapeDtypeStruct((64, 8192 + CODE), BF)
WIDE = pltpu.VMEM((64, 8192), BF)
WIDE_F = pltpu.VMEM((64, 8192), F32)
CODED = pltpu.VMEM((64, 8192 + CODE), BF)
SMALL = [pltpu.VMEM((64, 256), F32), pltpu.VMEM((64, 128), F32)]
PARAMS = pltpu.CompilerParams(vmem_limit_bytes=VMEM_LIMIT)
COST = pl.CostEstimate(flops=4 * 64 * 8192 * 256, bytes_accessed=16 * 1024 * 1024, transcendentals=0)


def forward(tick, table, fa, stores, weights, arrived, held):
    fresh = not arrived
    extra = tuple(arrived)
    n = 5 + len(extra) + len(weights)
    return pl.pallas_call(
        lambda *refs: forward_kernel(tick, fresh, *refs),
        out_shape=(BIG, BIG, PRE, INV, PK) + ((HELD, HELD) if fresh else ()),
        in_specs=[smem_spec()] * 2 + [hbm_spec()] + [weight_spec(), hbm_spec()] + [any_spec()] * len(extra)
        + [any_spec() if fresh else weight_spec()] * len(weights) + [hbm_spec()] * len(held),
        out_specs=[hbm_spec()] * 4 + [weight_spec()] + [weight_spec()] * (2 * fresh),
        scratch_shapes=[CODED, WIDE, WIDE, WIDE_F, WIDE] + SMALL
        + [pltpu.SemaphoreType.DMA((8 + 2 * PIECES,))],
        input_output_aliases={n + i: i for i in range(len(held))},
        compiler_params=PARAMS,
        cost_estimate=COST,
        name="section_forward",
    )(table, fa, *in_hbm(stores[0]), stores[1], *in_hbm(stores[2]), *extra, *weights, *held)


def backward(tick, table, fa, cot, weights, arrived, saved, held):
    fresh = not arrived
    extra = tuple(arrived)
    n = 3 + len(extra) + len(weights)
    return pl.pallas_call(
        lambda *refs: backward_kernel(tick, fresh, *refs),
        out_shape=(BIG, PRE, INV, BIG, BIG, GP, GP, PK),
        in_specs=[smem_spec()] * 2 + [hbm_spec()] + [any_spec()] * len(extra)
        + [weight_spec()] * len(weights) + [hbm_spec()] * (3 + len(held)),
        out_specs=[hbm_spec()] * 7 + [weight_spec()],
        scratch_shapes=[CODED, WIDE, WIDE_F, WIDE] + SMALL
        + [pltpu.VMEM((64, 256), BF)] * 2 + [pltpu.SemaphoreType.DMA((8,))],
        input_output_aliases={n + i: i for i in range(3 + len(held))},
        compiler_params=PARAMS,
        cost_estimate=COST,
        name="section_backward",
    )(table, fa, *in_hbm(cot), *extra, *weights, *saved, *held)


def transpose_kernel(wd, wu, wd_t, wu_t):
    for k in range(NF):
        wd_t[k] = wd[k].T
        wu_t[k] = wu[k].T


def transposed(weights):
    return pl.pallas_call(
        transpose_kernel,
        out_shape=(HELD,) * len(weights),
        in_specs=[weight_spec()] * len(weights),
        out_specs=[weight_spec()] * len(weights),
        compiler_params=PARAMS,
        cost_estimate=pl.CostEstimate(flops=0, bytes_accessed=16 * 1024 * 1024, transcendentals=0),
        name="transpose_weights",
    )(*weights)


def staged(store, after):
    def kernel(store_ref, _, store_v, sem):
        copy = pltpu.make_async_copy(store_ref, store_v, sem)
        copy.start()
        copy.wait()

    return pl.pallas_call(
        kernel,
        out_shape=pltpu.VMEM(BIG.shape, BF),
        in_specs=[hbm_spec(), any_spec()],
        out_specs=weight_spec(),
        scratch_shapes=[pltpu.SemaphoreType.DMA],
        compiler_params=PARAMS,
        name="stage_store",
    )(*in_hbm(store), after)


def prepare(down, up, gain):
    def kernel(down_ref, up_ref, gain_ref, out_ref):
        column = jnp.broadcast_to(gain_ref[...].astype(F32), (BLK, BLK)).T
        out_ref[pl.ds(0, BLK), :] = (column * down_ref[0].astype(F32)).astype(BF)
        out_ref[pl.ds(BLK, BLK), :] = up_ref[0]

    return pl.pallas_call(
        kernel,
        out_shape=jax.ShapeDtypeStruct((2 * BLK, BLK), BF),
        in_specs=[weight_spec()] * 3,
        out_specs=weight_spec(),
        name="scale_weights",
    )(down, up, gain)


def finish(terms, down, gain):
    def kernel(here, there, down_ref, gain_ref, gain_out, down_out, up_out):
        def total(rows):
            return here[0, rows, :].astype(F32) + there[0, rows, :].astype(F32)

        unit_t = total(pl.ds(0, BLK))
        up_out[0] = total(pl.ds(BLK, BLK))
        gain_out[...] = jnp.sum(down_ref[0].astype(F32).T * unit_t, axis=0, keepdims=True)
        down_out[0] = (unit_t * gain_ref[...].astype(F32)).T

    return pl.pallas_call(
        kernel,
        out_shape=(
            jax.ShapeDtypeStruct((1, BLK), F32),
            jax.ShapeDtypeStruct((1, BLK, BLK), F32),
            jax.ShapeDtypeStruct((1, BLK, BLK), F32),
        ),
        in_specs=[weight_spec()] * 4,
        out_specs=[weight_spec()] * 3,
        name="finish_gradients",
    )(*terms, down, gain)


EARLY = ((2, 0), (2, 1), (1, 1), (3, 0))
LATE = ((1, 0), (3, 1), (0, 0), (0, 1))


def partial_kernel(parts, pos, x_hbm, g_hbm, hs_hbm, gs_hbm, *refs):
    outs, (x_v, g_v, hs_v, gs_v, ht_v, gt_v, out_v, sems, osems) = refs[:4], refs[4:]
    loads = []
    for i, (src, dst) in enumerate(((gs_hbm, gs_v), (hs_hbm, hs_v), (x_hbm, x_v), (g_hbm, g_v))):
        cp = pltpu.make_async_copy(src, dst, sems.at[i])
        cp.start()
        loads.append(cp)
    z, x, y, odd = pos[0], pos[1], pos[2], pos[3]
    loads[0].wait()
    loads[1].wait()
    ht_v[...] = hs_v[...].astype(F32).T.astype(BF)
    gt_v[...] = gs_v[...].astype(F32).T.astype(BF)
    loads[2].wait()
    loads[3].wait()
    stores = []
    for n, (step, half) in enumerate(parts):
        for e in range(4):
            other, kz = 2 * half + e // 2, e % 2
            dx, dy = step + odd * (other - step), other + odd * (step - other)
            c = cols(lax.rem(z + kz, NZ) * (NX * NY) + lax.rem(x + dx, NX) * NY + lax.rem(y + dy, NY))
            out_v[n, e, pl.ds(0, BLK), :] = jnp.dot(gt_v[...], x_v[:, c], preferred_element_type=F32).astype(BF)
            out_v[n, e, pl.ds(BLK, BLK), :] = jnp.dot(ht_v[...], g_v[:, c], preferred_element_type=F32).astype(BF)
        cp = pltpu.make_async_copy(out_v.at[n], outs[n], osems.at[n])
        cp.start()
        stores.append(cp)
    for cp in stores:
        cp.wait()


def partials(parts, pos, x_all, g_all, hs_all, gs_all):
    rows, width = x_all.shape
    group = jax.ShapeDtypeStruct((4, 2 * BLK, BLK), BF)
    outs = pl.pallas_call(
        lambda *refs: partial_kernel(parts, *refs),
        out_shape=(group,) * 4,
        in_specs=[smem_spec()] + [hbm_spec()] * 4,
        out_specs=[any_spec()] * 4,
        scratch_shapes=[pltpu.VMEM((rows, width), BF)] * 2
        + [pltpu.VMEM((rows, 256), BF)] * 2
        + [pltpu.VMEM((256, rows), BF)] * 2
        + [pltpu.VMEM((4, 4, 2 * BLK, BLK), BF)]
        + [pltpu.SemaphoreType.DMA((4,)), pltpu.SemaphoreType.DMA((4,))],
        compiler_params=PARAMS,
        cost_estimate=pl.CostEstimate(
            flops=2 * rows * width * 256, bytes_accessed=10 * 1024 * 1024, transcendentals=0
        ),
        name="gradient_partials",
    )(pos, x_all, g_all, hs_all, gs_all)
    return dict(zip(parts, outs))


def gather_weights(own):
    pair = jnp.stack([own, shift(own, 1, 0, 0)])
    two, one, three = [shift(pair, *along(-d)) for d in (2, 1, 3)]
    lo, hi = jnp.concatenate([pair, one], axis=0), jnp.concatenate([three, two], axis=0)
    ahead_lo, behind_lo = shift(lo, *across(-1)), shift(lo, *across(1))
    behind_hi, ahead_hi = shift(hi, *across(1)), shift(hi, *across(-1))
    far_lo, far_hi = shift(ahead_lo, *across(-1)), shift(behind_hi, *across(1))
    low, high = (0, 1), (3, 2)
    places = [
        (kz, d, e)
        for e, ds in ((0, low), (1, low), (3, low), (0, high), (3, high), (1, high), (2, low), (2, high))
        for d in ds
        for kz in range(NZ)
    ]
    return places, (lo, ahead_lo, behind_lo, hi, behind_hi, ahead_hi, far_lo, far_hi), pair


LAG = (0, 1, 3, 4)
SOURCE = (0, 1, 2, 1)
ORDER = (
    [("forward", t) for t in range(4)]
    + [("transpose", 0)]
    + [(kind, t + 4 * (kind == "forward")) for t in range(3) for kind in ("forward", "backward")]
    + [("backward", t) for t in range(3, 7)]
)


def place(keys, z, x, y, odd):
    keys = jnp.array(keys, jnp.int32)
    dx, dy = jnp.where(odd, keys[:, 2], keys[:, 1]), jnp.where(odd, keys[:, 1], keys[:, 2])
    return (lax.rem(z + keys[:, 0], NZ) * (NX * NY) + lax.rem(x + dx, NX) * NY + lax.rem(y + dy, NY)).astype(jnp.int32)


def add_up(*terms):
    return sum(t.astype(F32) for t in terms).astype(BF)


def scatter(part):
    far_lo, far_hi = shift(part[2, 0], *along(1)), shift(part[2, 1], *along(-1))
    up_hi, down_lo = shift(part[1, 1], *along(1)), shift(part[3, 0], *along(-1))
    up_lo = shift(add_up(part[1, 0], far_lo), *along(1))
    down_hi = shift(add_up(part[3, 1], far_hi), *along(-1))
    low = (part[0, 0], up_lo, down_lo)
    high = (part[0, 1], up_hi, down_hi)
    far = shift(add_up(*(t[0:2] for t in high)), *across(2))
    behind = shift(add_up(*(t[2:4] for t in high)), *across(-1))
    ahead = shift(add_up(*(t[2:4] for t in low)), *across(1))
    own = [t[0:2] for t in low]
    there = shift(add_up(*(t[1:2] for t in own), ahead[1:2], far[1:2], behind[1:2]), 1, 0, 0)
    here = add_up(*(t[0:1] for t in own), ahead[0:1], far[0:1], behind[0:1])
    return here, there


def per_device(entering, in_store, out_store, norm_gain, adapter_down, adapter_up, sample_ids, cotangent):
    n_sec = lax.axis_size("pipe")
    sec = lax.axis_index("pipe")
    f = lax.axis_index("fsdp")
    z, x, y = f // (NX * NY), lax.rem(f // NY, NX), lax.rem(f, NY)
    n_micro, rows, width = entering.shape

    odd = lax.rem(sec, 2)
    keys, weights, pair = gather_weights(prepare(adapter_down, adapter_up, norm_gain))
    fa = place(keys, z, x, y, odd == 1)

    lag = jnp.array(LAG, jnp.int32)
    ticks = n_micro + LAG[-1]
    step = jnp.arange(ticks, dtype=jnp.int32)
    m_f, m_b = step - lag[sec], step - lag[n_sec - 1 - sec]
    slot_f, slot_b = jnp.clip(m_f, 0, n_micro - 1), jnp.clip(m_b, 0, n_micro - 1)
    source_f, source_b = jnp.array(SOURCE, jnp.int32)[sec], jnp.array(SOURCE, jnp.int32)[n_sec - 1 - sec]
    table = jnp.stack(
        [
            (m_f >= 0) & (m_f < n_micro),
            slot_f,
            sample_ids[slot_f],
            jnp.broadcast_to(source_f, (ticks,)),
            (m_b >= 0) & (m_b < n_micro),
            slot_b,
            jnp.broadcast_to(source_b, (ticks,)),
            step,
        ],
        axis=1,
    ).astype(jnp.int32)

    def send(block, tick, hops, towards):
        edges = [hop[::towards] for hop in hops]
        live = [e for e in edges if 0 <= tick - LAG[e[0] if towards == 1 else n_sec - 1 - e[0]] < n_micro]
        return lax.ppermute(block, "pipe", live) if live else None

    def arrivals(near, far, tick):
        pair = (near.get(tick - 1), far.get(tick - 2))
        return tuple(p if p is not None else q for p, q in (pair, pair[::-1]) if p is not None or q is not None)

    stores = (entering, staged(in_store[0], pair), out_store[0])
    near_f, far_f, near_b, far_b = {}, {}, {}, {}
    held_f, held_b = (), ()
    weights_t = None
    for kind, tick in ORDER:
        if kind == "transpose":
            weights_t = transposed(weights)
        elif kind == "forward":
            *held_f, sent = forward(tick, table, fa, stores, weights, arrivals(near_f, far_f, tick), held_f)
            if tick == 0:
                *held_f, sent, wd_all, wu_all = (*held_f, sent)
                weights = (wd_all, wu_all)
            near_f[tick] = send(sent, tick, ((0, 1), (2, 3)), 1)
            far_f[tick] = send(sent, tick, ((1, 2),), 1)
        else:
            ib, sb, pb, vb = held_f
            ib, pb, vb, *held_b, back = backward(
                tick, table, fa, cotangent, weights_t, arrivals(near_b, far_b, tick), (ib, pb, vb), held_b
            )
            held_f = (ib, sb, pb, vb)
            near_b[tick] = send(back, tick, ((0, 1), (2, 3)), -1)
            far_b[tick] = send(back, tick, ((1, 2),), -1)
    ib, sb, pb, vb = held_f
    gb, xb, hb, qb = held_b

    all_rows = n_micro * rows
    pos = jnp.stack([z, x, y, odd]).astype(jnp.int32)
    whole = [t.reshape(all_rows, -1) for t in (ib, gb, hb, qb)]
    parts = {**partials(EARLY, pos, *whole), **partials(LATE, pos, *whole)}
    grad_gain, grad_down, grad_up = finish(scatter(parts), adapter_down, norm_gain)
    return (
        sb[None],
        ib[None],
        xb[None],
        grad_gain,
        grad_down,
        grad_up,
    )


def solution(mesh):
    return jax.shard_map(
        per_device,
        mesh=mesh,
        in_specs=(
            P(None, "fsdp", None),
            P("pipe", None, "fsdp", None),
            P("pipe", None, "fsdp", None),
            P("pipe", "fsdp"),
            P("pipe", "fsdp", None),
            P("pipe", None, "fsdp"),
            P(),
            P(None, "fsdp", None),
        ),
        out_specs=(
            P("pipe", None, "fsdp", None),
            P("pipe", None, "fsdp", None),
            P("pipe", None, "fsdp", None),
            P("pipe", "fsdp"),
            P("pipe", "fsdp", None),
            P("pipe", None, "fsdp"),
        ),
        check_vma=False,
    )
```
